32 devices in a mesh: beam: 8 (over y, x, core), trans: 4 (over z).
Axes of the slice: x: 2, y: 2, z: 4, core: 2. Of those that a mesh axis runs over, the one named last changes fastest.
Arguments:
- field_in: float32 [2, 32, 256, 256], P(None, 'beam', 'trans'), may hold values from -4 to 4
- phases: float32 [32, 4096], P('beam'), may hold values from -3.140625 to 3.140625
- energy: float32 [32, 4096], P('beam'), may hold values from -3 to 3
- row_cell: int32 [32, 4096], P('beam'), may hold values from 32 to 223
- col_cell: int32 [32, 4096], P('beam'), may hold values from 32 to 223
- weight: int32 [32, 4096], P('beam'), may hold values from 1 to 15
- charge: int32 [32], P('beam'), may hold values from 256 to 1024
- pole_rate: float32 [8], replicated, may hold values from 0.0078125 to 0.5
- pole_freq: float32 [8], replicated, may hold values from 0 to 0.3
- pole_amp: float32 [8], replicated, may hold values from -3 to 3
Outputs:
- field_out: float32 [2, 32, 256, 256], P(None, 'beam', 'trans')
- phase_out: float32 [32, 4096], P('beam')
- energy_out: float32 [32, 4096], P('beam')
The draws below stay inside these ranges and needn't reach their ends.
All inputs are finite; a program needn't handle non-finite values.
Results may differ from the reference program's by a relative error of at most 0.00042.
Values sent between devices are 32-bit elements; how exact they have to be, the bound alone decides.
A program may use at most 64 MiB of HBM per device.

```python
import math
import jax
import jax.numpy as jnp
from jax import lax

GRID = 256
NPART = 4096
POLES = 8
PERIODS = 2
SLICES = 32


def with_ends(values, key, least, largest):
    dims = values.shape
    spot = [jax.random.randint(jax.random.fold_in(key, axis), (), 0, dims[axis]) for axis in range(len(dims))]
    values = values.at[tuple(spot)].set(least)
    longest = dims.index(max(dims))
    spot[longest] = (spot[longest] + 1) % dims[longest]
    return values.at[tuple(spot)].set(largest)


def block_scale(own_key, shape, shards, least, top_value):
    loudness, own = 1.0, jax.random.fold_in(own_key, 6)
    for dim, parts in shards:
        steps = jnp.exp(jax.random.uniform(jax.random.fold_in(own, dim), (parts,), jnp.float32, least / len(shards), top_value / len(shards)))
        loudness = loudness * jnp.repeat(steps, shape[dim] // parts).reshape([-1 if axis == dim else 1 for axis in range(len(shape))])
    return loudness


def scatter_about(rng, shape, spread, reach, split=(), held_as=jnp.bfloat16):
    factor_of = block_scale(rng, shape, split, -0.22, 0.18) if split else 1.0
    drawn = jax.random.normal(rng, shape, jnp.float32) * spread * factor_of
    return jnp.minimum(jnp.maximum(drawn, -reach), reach).astype(held_as)


def setup_inputs(seed: int = 0) -> dict:
    splits = jax.random.split(jax.random.key(seed), 11)
    field_in = scatter_about(splits[0], (2, SLICES, GRID, GRID), 0.5, 4.0, ((1, 8), (2, 4)), jnp.float32)
    phases = jnp.clip(jax.random.uniform(splits[1], (SLICES, NPART), jnp.float32, -3.140625, 3.140625), -3.140625, 3.140625)
    energy = scatter_about(splits[2], (SLICES, NPART), 0.5, 3.0, ((0, 8),), jnp.float32)
    row_cell = with_ends(jax.random.randint(splits[3], (SLICES, NPART), GRID // 8, GRID - GRID // 8), jax.random.fold_in(splits[3], 1), GRID // 8, (GRID - GRID // 8) - 1).astype(jnp.int32)
    col_cell = with_ends(jax.random.randint(splits[4], (SLICES, NPART), GRID // 8, GRID - GRID // 8), jax.random.fold_in(splits[4], 1), GRID // 8, (GRID - GRID // 8) - 1).astype(jnp.int32)
    weight = with_ends(jax.random.randint(splits[5], (SLICES, NPART), 1, 16), jax.random.fold_in(splits[5], 1), 1, 15).astype(jnp.int32)
    charge = with_ends(jax.random.randint(splits[6], (SLICES,), 256, 1025), jax.random.fold_in(splits[6], 1), 256, 1024).astype(jnp.int32)
    pole_rate = jnp.clip(jnp.exp(jax.random.uniform(splits[7], (POLES,), jnp.float32, math.log(0.0078125), math.log(0.5))), 0.0078125, 0.5)
    pole_freq = jnp.clip(jax.random.uniform(splits[8], (POLES,), jnp.float32, 0.0, 0.3), 0.0, 0.3)
    pole_amp = scatter_about(splits[9], (POLES,), 0.5, 3.0, (), jnp.float32)
    return dict(field_in=field_in, phases=phases, energy=energy, row_cell=row_cell, col_cell=col_cell, weight=weight, charge=charge, pole_rate=pole_rate, pole_freq=pole_freq, pole_amp=pole_amp)


diffraction = 20.0
kick_gain = 0.5
deposit_gain = 0.05
wake_gain = 3.0
charge_unit = 1024.0


def wake_profile(charge_norm, pole_rate, pole_freq, pole_amp):
    damping = jnp.exp(-pole_rate)
    step_re = damping * jnp.cos(pole_freq)
    step_im = damping * jnp.sin(pole_freq)

    def advance(state, amount):
        state_re, state_im = state
        loaded = state_re + amount
        advanced = (step_re * loaded - step_im * state_im, step_im * loaded + step_re * state_im)
        return advanced, state_re

    initial = (jnp.zeros_like(pole_rate), jnp.zeros_like(pole_rate))
    ending, history = lax.scan(advance, initial, charge_norm)
    summed = jnp.sum(pole_amp[None, :] * (history + 0.5 * charge_norm[:, None]), axis=1)
    return (wake_gain / SLICES) * summed


def reference(field_in, phases, energy, row_cell, col_cell, weight, charge, pole_rate, pole_freq, pole_amp):
    charge_norm = charge.astype(jnp.float32) / charge_unit
    wake_kick = wake_profile(charge_norm, pole_rate, pole_freq, pole_amp)
    freq_index = jnp.arange(GRID, dtype=jnp.int32)
    centred = ((freq_index + GRID // 2) % GRID - GRID // 2).astype(jnp.float32) / GRID
    kernel_phase = diffraction * (centred[:, None] ** 2 + centred[None, :] ** 2)
    propagator = jnp.cos(kernel_phase) - 1j * jnp.sin(kernel_phase)
    slice_ids = jnp.arange(SLICES, dtype=jnp.int32)[:, None]
    weights = weight.astype(jnp.float32)
    wavefront = field_in[0] + 1j * field_in[1]
    angles = phases
    energies = energy
    for period in range(PERIODS):
        probed = wavefront[slice_ids, row_cell, col_cell]
        energies = energies - kick_gain * (jnp.real(probed) * jnp.cos(angles) - jnp.imag(probed) * jnp.sin(angles)) - wake_kick[:, None]
        angles = angles + energies
        bunch_re = lax.optimization_barrier((weights * jnp.cos(angles)).astype(jnp.bfloat16)).astype(jnp.float32)
        bunch_im = lax.optimization_barrier((-weights * jnp.sin(angles)).astype(jnp.bfloat16)).astype(jnp.float32)
        empty = jnp.zeros((SLICES, GRID, GRID), jnp.float32)
        grid_re = empty.at[slice_ids, row_cell, col_cell].add(bunch_re)
        grid_im = empty.at[slice_ids, row_cell, col_cell].add(bunch_im)
        wavefront = wavefront + (deposit_gain * charge_norm)[:, None, None] * (grid_re + 1j * grid_im)
        spectrum = jnp.fft.fft2(wavefront, norm="ortho") * propagator
        wavefront = jnp.fft.ifft2(spectrum, norm="ortho")
        wavefront = jnp.concatenate([jnp.zeros_like(wavefront[:1]), wavefront[:-1]], axis=0)
    field_out = jnp.stack([jnp.real(wavefront), jnp.imag(wavefront)])
    return field_out, angles, energies
```

```python
import functools
import math

import jax
import jax.numpy as jnp
import ml_dtypes
import numpy as np
from jax import lax
from jax.experimental import pallas as pl
from jax.experimental.pallas import tpu as pltpu
from jax.sharding import PartitionSpec as P

PERIODS = 2


diffraction = 20.0
kick_gain = 0.5
deposit_gain = 0.05
wake_gain = 3.0
charge_unit = 1024.0


def shifted(value, axis, steps):
    count = lax.axis_size(axis)
    first, last = (max(0, -steps), min(count, count - steps))
    return lax.ppermute(value, axis, [(source, source + steps) for source in range(first, last)])


def complex_product(form, left_re, left_im, right_re, right_im):

    def single(first, second):
        return jnp.einsum(form, first, second, precision=lax.Precision.HIGHEST)

    return (
        single(left_re, right_re) - single(left_im, right_im),
        single(left_re, right_im) + single(left_im, right_re),
    )


def dft_table(length, sign):
    counter = jnp.arange(length, dtype=jnp.int32)
    product = counter[:, None] * counter[None, :] % length
    radians = 2.0 * math.pi / length * product.astype(jnp.float32)
    factor = 1.0 / math.sqrt(length)
    return (jnp.cos(radians) * factor, sign * jnp.sin(radians) * factor)


def propagator(row_index, col_index, length):

    def centred(index):
        return ((index + length // 2) % length - length // 2).astype(jnp.float32) / length

    radians = diffraction * (centred(row_index) ** 2 + centred(col_index) ** 2)
    return (jnp.cos(radians), -jnp.sin(radians))


def pole_power(steps, pole_rate, pole_freq):
    damping = jnp.exp(-pole_rate * steps)
    radians = pole_freq * steps
    return (damping * jnp.cos(radians), damping * jnp.sin(radians))


def wake_kicks(charge, pole_rate, pole_freq, pole_amp):
    members = charge.shape[0]
    groups = lax.axis_size("beam")
    position = lax.axis_index("beam")
    charge_norm = charge.astype(jnp.float32) / charge_unit
    offsets = jnp.arange(members, dtype=jnp.float32)
    distance = offsets[:, None] - offsets[None, :]
    inner_re, inner_im = pole_power(jnp.maximum(distance, 0.0)[..., None], pole_rate, pole_freq)
    before = (distance > 0.0)[..., None]
    local_re = jnp.sum(jnp.where(before, inner_re, 0.0) * charge_norm[None, :, None], axis=1)
    tail_re, tail_im = pole_power((members - offsets)[:, None], pole_rate, pole_freq)
    block_re = jnp.sum(charge_norm[:, None] * tail_re, axis=0)
    block_im = jnp.sum(charge_norm[:, None] * tail_im, axis=0)
    gathered_re, gathered_im = (
        lax.all_gather(block_re[None, :], "beam", axis=0, tiled=True),
        lax.all_gather(block_im[None, :], "beam", axis=0, tiled=True),
    )
    sources = jnp.arange(groups, dtype=jnp.int32)
    spacing = (position - 1 - sources).astype(jnp.float32) * members
    reach_re, reach_im = pole_power(jnp.maximum(spacing, 0.0)[:, None], pole_rate, pole_freq)
    valid = (sources < position)[:, None]
    carry_re = jnp.sum(
        jnp.where(valid, gathered_re * reach_re - gathered_im * reach_im, 0.0), axis=0
    )
    carry_im = jnp.sum(
        jnp.where(valid, gathered_re * reach_im + gathered_im * reach_re, 0.0), axis=0
    )
    lead_re, lead_im = pole_power(offsets[:, None], pole_rate, pole_freq)
    state_re = local_re + lead_re * carry_re[None, :] - lead_im * carry_im[None, :]
    summed = jnp.sum(pole_amp[None, :] * (state_re + 0.5 * charge_norm[:, None]), axis=1)
    return wake_gain / (members * groups) * summed


def deposit_slice(band_rows, grid_cols, operands):
    local_row, column, part_re, part_im = operands
    row_hot = (local_row[:, None] == jnp.arange(band_rows, dtype=jnp.int32)[None, :]).astype(
        jnp.bfloat16
    )
    col_hot = (column[:, None] == jnp.arange(grid_cols, dtype=jnp.int32)[None, :]).astype(
        jnp.bfloat16
    )
    spread = jnp.concatenate([col_hot * part_re[:, None], col_hot * part_im[:, None]], axis=1)
    return lax.dot_general(
        row_hot, spread, (((0,), (0,)), ((), ())), preferred_element_type=jnp.float32
    )


def probe_slice(band_rows, grid_cols, operands):
    local_row, column, slab_re, slab_im = operands
    row_hot = (local_row[:, None] == jnp.arange(band_rows, dtype=jnp.int32)[None, :]).astype(
        jnp.float32
    )
    stacked = jnp.concatenate([slab_re, slab_im], axis=1)
    picked = jnp.dot(
        row_hot, stacked, precision=lax.Precision.HIGHEST, preferred_element_type=jnp.float32
    )
    col_hot = column[:, None] == jnp.arange(grid_cols, dtype=jnp.int32)[None, :]
    value_re = jnp.sum(jnp.where(col_hot, picked[:, :grid_cols], 0.0), axis=1)
    value_im = jnp.sum(jnp.where(col_hot, picked[:, grid_cols:], 0.0), axis=1)
    return (value_re, value_im)


def diffract(field_re, field_im, forward, inverse):
    cols_re, cols_im = complex_product("srn,nc->scr", field_re, field_im, forward[0], forward[1])
    halves = lax.all_to_all(
        jnp.stack([cols_re, cols_im]), "trans", split_axis=2, concat_axis=3, tiled=True
    )
    part_re = halves[0]
    part_im = halves[1]
    col_band = part_re.shape[1]
    grid_rows = part_re.shape[2]
    columns = lax.axis_index("trans") * col_band + jnp.arange(col_band, dtype=jnp.int32)
    spec_re, spec_im = complex_product("sqr,rk->sqk", part_re, part_im, forward[0], forward[1])
    kernel_re, kernel_im = propagator(
        jnp.arange(grid_rows, dtype=jnp.int32)[None, :], columns[:, None], grid_rows
    )
    moved_re = spec_re * kernel_re - spec_im * kernel_im
    moved_im = spec_re * kernel_im + spec_im * kernel_re
    back_re, back_im = complex_product("sqk,kr->sqr", moved_re, moved_im, inverse[0], inverse[1])
    rows_both = lax.all_to_all(
        jnp.stack([back_re, back_im]), "trans", split_axis=3, concat_axis=2, tiled=True
    )
    return complex_product("scr,cn->srn", rows_both[0], rows_both[1], inverse[0], inverse[1])


def shards(
    field_in, phases, energy, row_cell, col_cell, weight, charge, pole_rate, pole_freq, pole_amp
):
    field_re = field_in[0]
    field_im = field_in[1]
    slab_count, band_rows, grid_cols = field_re.shape
    row_start = lax.axis_index("trans") * band_rows
    wake_kick = wake_kicks(charge, pole_rate, pole_freq, pole_amp)
    charge_norm = charge.astype(jnp.float32) / charge_unit
    strength = (deposit_gain * charge_norm)[:, None, None]
    local_row = row_cell - row_start
    weights = weight.astype(jnp.float32)
    forward = dft_table(grid_cols, -1.0)
    inverse = dft_table(grid_cols, 1.0)
    depositor = functools.partial(deposit_slice, band_rows, grid_cols)
    reader = functools.partial(probe_slice, band_rows, grid_cols)
    angles = phases
    energies = energy
    for period in range(PERIODS):
        local_re, local_im = lax.map(reader, (local_row, col_cell, field_re, field_im))
        probed = lax.psum(jnp.stack([local_re, local_im]), "trans")
        energies = (
            energies
            - kick_gain * (probed[0] * jnp.cos(angles) - probed[1] * jnp.sin(angles))
            - wake_kick[:, None]
        )
        angles = angles + energies
        part_re = (weights * jnp.cos(angles)).astype(jnp.bfloat16)
        part_im = (-weights * jnp.sin(angles)).astype(jnp.bfloat16)
        bunched = lax.map(depositor, (local_row, col_cell, part_re, part_im))
        field_re = field_re + strength * bunched[:, :, :grid_cols]
        field_im = field_im + strength * bunched[:, :, grid_cols:]
        field_re, field_im = diffract(field_re, field_im, forward, inverse)
        head_slice = shifted(jnp.stack([field_re[-1], field_im[-1]]), "beam", 1)
        field_re = jnp.concatenate([head_slice[0][None], field_re[:-1]], axis=0)
        field_im = jnp.concatenate([head_slice[1][None], field_im[:-1]], axis=0)
    return (jnp.stack([field_re, field_im]), angles, energies)


MESH = pl.DeviceIdType.MESH
LANES = 128
SUBLANES = 8
F32 = jnp.float32
BF16 = jnp.bfloat16


def one_axis_propagator(length):
    index = np.arange(length)
    centred = ((index + length // 2) % length - length // 2) / length
    ring = np.fft.ifft(np.exp(-1j * diffraction * centred**2))
    full = ring[(index[:, None] - index[None, :]) % length]
    block = np.block([[full.real, -full.imag], [full.imag, full.real]]).astype(np.float32)
    upper = block.astype(ml_dtypes.bfloat16)
    lower = (block - upper.astype(np.float32)).astype(ml_dtypes.bfloat16)
    return np.stack([upper, lower])


def two_parts(value):
    upper = value.astype(BF16)
    return upper, (value - upper.astype(F32)).astype(BF16)


def mm(left, right):
    return jnp.dot(left, right, preferred_element_type=F32)


def mm_t(left, right):
    return lax.dot_general(left, right, (((1,), (1,)), ((), ())), preferred_element_type=F32)


def slices_kernel(
    groups,
    field_in, phases, energy, row_cell, col_cell, weight, charge, pole_rate, pole_freq, pole_amp, table,
    field_out, phase_out, energy_out,
    field, moved, taps, cells, state, result, arrived, probes, parts, halves, col_hot, row_hot, charges, charge_tile,
    field_send, field_recv, cell_send, cell_recv, state_send, state_recv, result_send, result_recv,
    out_send, out_recv, charge_send, charge_recv, local_sems,
):
    beam, trans = lax.axis_index("beam"), lax.axis_index("trans")
    members, band, cols = field_in.shape[1:]
    rows = members * band
    total = groups * members
    width = phases.shape[1] // SUBLANES
    edge = rows // 8
    inner = rows - 2 * edge
    mine = beam * members + trans
    ahead, behind = lax.rem(beam + 1, groups), lax.rem(beam + groups - 1, groups)

    barrier = pltpu.get_barrier_semaphore()

    def greet(beam_to, trans_to):
        pl.semaphore_signal(barrier, inc=1, device_id=(beam_to, trans_to), device_id_type=MESH)

    for step in range(1, members):
        greet(beam, lax.rem(trans + step, members))
    for step in range(1, groups):
        greet(lax.rem(beam + step, groups), trans)
    for source in (members - 2, members - 1):
        @pl.when(trans != source)
        def _():
            greet(behind, source)

    @pl.when(trans == members - 1)
    def _():
        greet(ahead, 0)

    take = pltpu.make_async_copy(field_in.at[:, trans], field.at[:, trans], local_sems.at[0])
    take.start()
    take_table = pltpu.make_async_copy(table, taps, local_sems.at[1])
    take_table.start()

    expected = (members - 1) + (groups - 1) + jnp.where(trans >= members - 2, members - 1, 0) + jnp.where(trans == 0, 1, 0)
    pl.semaphore_wait(barrier, expected)

    def remote(source, target, send, recv, beam_to, trans_to):
        return pltpu.make_async_remote_copy(
            src_ref=source, dst_ref=target, send_sem=send, recv_sem=recv,
            device_id=(beam_to, trans_to), device_id_type=MESH,
        )

    field_copies = []
    for step in [members - 1 - k for k in range(members - 1)]:
        to = lax.rem(trans + step, members)
        copy = remote(field_in.at[:, to], field.at[:, trans], field_send.at[step], field_recv.at[trans], beam, to)
        copy.start()
        field_copies.append(copy)

    lane = lax.broadcasted_iota(jnp.int32, charge_tile.shape, 1)
    own = jnp.zeros(charge_tile.shape, F32)
    for k in range(members):
        own = jnp.where(lane == beam * members + k, charge[k].astype(F32) / charge_unit, own)
    charge_tile[...] = own
    charges[pl.ds(beam, 1)] = own[None]
    charge_copies = []
    for step in range(1, groups):
        copy = remote(charge_tile, charges.at[beam], charge_send.at[step], charge_recv.at[beam], lax.rem(beam + step, groups), trans)
        copy.start()
        charge_copies.append(copy)

    for k in range(SUBLANES):
        here = pl.ds(k * width, width)
        for place, source in enumerate((row_cell, col_cell, weight)):
            cells[0, place, k : k + 1, :] = source[pl.ds(trans, 1), here].astype(F32)
        state[0, 0, k : k + 1, :] = phases[pl.ds(trans, 1), here]
        state[0, 1, k : k + 1, :] = energy[pl.ds(trans, 1), here]
    first = trans == 0
    prior_beam = jnp.where(first, behind, beam)
    prior_trans = jnp.where(first, members - 1, trans - 1)
    cell_copy = remote(cells.at[0], cells.at[1], cell_send, cell_recv, prior_beam, prior_trans)
    cell_copy.start()

    def one_hots(period):
        col_index = lax.broadcasted_iota(jnp.int32, (cols, width), 0).astype(F32)

        def body(k, carry):
            col_hot[period, k] = jnp.where(cells[period, 1, pl.ds(k, 1), :] == col_index, 1.0, 0.0).astype(BF16)
            return carry

        lax.fori_loop(0, SUBLANES, body, 0)

    one_hots(0)

    for step in range(1, groups):
        source = lax.rem(beam + step, groups)
        remote(charge_tile, charges.at[source], charge_send.at[step], charge_recv.at[source], source, trans).wait_recv()
    every = jnp.sum(charges[...], axis=0)

    def wake_and_charge(slice_id):
        distance = slice_id - lane
        ago = jnp.maximum(distance, 0).astype(F32)
        memory = jnp.zeros(lane.shape, F32)
        amount = F32(0)
        for k in range(pole_rate.shape[0]):
            memory = memory + pole_amp[k] * (jnp.exp(-pole_rate[k] * ago) * jnp.cos(pole_freq[k] * ago))
            amount = amount + pole_amp[k]
        memory = jnp.where(distance > 0, memory, jnp.where(distance == 0, 0.5 * amount, 0.0))
        wake = (wake_gain / total) * jnp.sum(memory * every, axis=1, keepdims=True)
        return wake, jnp.sum(jnp.where(distance == 0, every, 0.0), axis=1, keepdims=True)

    following = lax.rem(mine + 1, total)
    wakes = [wake_and_charge(mine), wake_and_charge(following)]
    cell_copy.wait_recv()
    one_hots(1)
    start_cos, start_sin = jnp.cos(state[0, 0]), jnp.sin(state[0, 0])

    take.wait()
    for step in range(1, members):
        source = lax.rem(trans + step, members)
        remote(field_in.at[:, source], field.at[:, source], field_send.at[step], field_recv.at[source], beam, source).wait_recv()
    take_table.wait()

    row_index = lax.broadcasted_iota(jnp.int32, (inner, width), 0).astype(F32) + float(edge)

    def push(period, cos_now, sin_now):
        flat = field[...].reshape(2, rows, cols)
        for part in range(2):
            upper, lower = two_parts(flat[part, edge : rows - edge])
            halves[0, part * inner : (part + 1) * inner, :] = upper
            halves[1, part * inner : (part + 1) * inner, :] = lower

        def body(k, carry):
            hot = col_hot[period, k]
            picked = mm(halves[0], hot) + mm(halves[1], hot)
            inside = cells[period, 0, pl.ds(k, 1), :] == row_index
            probes[0, pl.ds(k, 1), :] = jnp.sum(jnp.where(inside, picked[:inner], 0.0), axis=0, keepdims=True)
            probes[1, pl.ds(k, 1), :] = jnp.sum(jnp.where(inside, picked[inner:], 0.0), axis=0, keepdims=True)
            return carry

        lax.fori_loop(0, SUBLANES, body, 0, unroll=True)
        eta = state[period, 1] - kick_gain * (probes[0] * cos_now - probes[1] * sin_now) - wakes[period][0]
        theta = state[period, 0] + eta
        return theta, eta

    def deposit_and_diffract(period, theta):
        heavy = cells[period, 2]
        parts[0] = (heavy * jnp.cos(theta)).astype(BF16).astype(F32)
        parts[1] = (-heavy * jnp.sin(theta)).astype(BF16).astype(F32)
        bunched = jnp.zeros((2 * inner, cols), F32)
        for k in range(SUBLANES):
            inside = cells[period, 0, k : k + 1, :] == row_index
            spread = jnp.concatenate(
                [jnp.where(inside, parts[part, k : k + 1, :], 0.0).astype(BF16) for part in range(2)], axis=0
            )
            row_hot[:, k * width : (k + 1) * width] = spread
            bunched = bunched + mm_t(row_hot[:, k * width : (k + 1) * width], col_hot[period, k])
        strength = deposit_gain * wakes[period][1][:1, :1]
        flat = field[...].reshape(2, rows, cols)
        wide = []
        for part in range(2):
            loaded = flat[part, edge : rows - edge] + strength * bunched[part * inner : (part + 1) * inner]
            wide.append(jnp.concatenate([flat[part, :edge], loaded, flat[part, rows - edge :]], axis=0))
        upper, lower = two_parts(jnp.concatenate(wide, axis=1))
        across = mm_t(upper, taps[0]) + (mm_t(lower, taps[0]) + mm_t(upper, taps[1]))
        upper, lower = two_parts(jnp.concatenate([across[:, :cols], across[:, cols:]], axis=0))
        return mm(taps[0], upper) + (mm(taps[0], lower) + mm(taps[1], upper))

    theta, eta = push(0, start_cos, start_sin)
    state[0, 0] = theta
    state[0, 1] = eta
    state_copy = remote(state.at[0], state.at[1], state_send, state_recv, prior_beam, prior_trans)
    state_copy.start()
    spread_field = deposit_and_diffract(0, theta)
    field[...] = jnp.where(following == 0, 0.0, spread_field).reshape(field.shape)

    state_copy.wait_recv()
    theta, eta = push(1, jnp.cos(state[1, 0]), jnp.sin(state[1, 0]))
    result[0] = theta
    result[1] = eta

    def scatter(shift, source_of, target, send, recv, sem):
        slot = lax.rem(trans + shift, members)
        stays = trans + shift < members
        beam_to = jnp.where(stays, beam, ahead)
        copies = []
        for step in [members // 2 + k for k in range(members - members // 2)] + list(range(1, members // 2)):
            to = lax.rem(trans + step, members)
            copy = remote(source_of(to), target(slot), send.at[step], recv.at[slot], beam_to, to)
            copy.start()
            copies.append(copy)
        away = remote(source_of(trans), target(slot), send.at[0], recv.at[slot], ahead, trans)
        here = pltpu.make_async_copy(source_of(trans), target(slot), sem)

        @pl.when(stays)
        def _():
            here.start()

        @pl.when(jnp.logical_not(stays))
        def _():
            away.start()

        def finish():
            for copy in copies:
                copy.wait_send()

            @pl.when(stays)
            def _():
                here.wait()

            @pl.when(jnp.logical_not(stays))
            def _():
                away.wait_send()

            for place in range(members):
                def wait_for():
                    remote(source_of(trans), target(place), send.at[0], recv.at[place], beam, trans).wait_recv()

                if place < shift:
                    wait_for()
                else:
                    pl.when(trans != place - shift)(wait_for)

        return finish

    finish_result = scatter(
        1, lambda to: result, lambda slot: arrived.at[slot], result_send, result_recv, local_sems.at[2]
    )
    spread_field = deposit_and_diffract(1, theta)
    moved[...] = jnp.where(lax.rem(mine + 2, total) == 0, 0.0, spread_field).reshape(moved.shape)
    finish_field = scatter(
        2, lambda to: moved.at[:, to], lambda slot: field_out.at[:, slot], out_send, out_recv, local_sems.at[3]
    )

    finish_result()
    for place in range(members):
        for k in range(SUBLANES):
            here = slice(k * width, (k + 1) * width)
            phase_out[place : place + 1, here] = arrived[place, 0, k : k + 1, :]
            energy_out[place : place + 1, here] = arrived[place, 1, k : k + 1, :]
    for copy in field_copies + charge_copies + [cell_copy, state_copy]:
        copy.wait_send()
    finish_field()


def whole_slices(
    field_in, phases, energy, row_cell, col_cell, weight, charge, pole_rate, pole_freq, pole_amp
):
    groups, members = lax.axis_size("beam"), lax.axis_size("trans")
    band, cols = field_in.shape[2:]
    rows = members * band
    inner = rows - 2 * (rows // 8)
    width = phases.shape[1] // SUBLANES
    lanes = -(-groups * members // LANES) * LANES
    table = jnp.asarray(one_axis_propagator(cols))
    vmem, smem, anywhere = (pl.BlockSpec(memory_space=space) for space in (pltpu.VMEM, pltpu.SMEM, pl.ANY))
    dma = pltpu.SemaphoreType.DMA
    return tuple(pl.pallas_call(
        functools.partial(slices_kernel, groups),
        out_shape=(
            jax.ShapeDtypeStruct(field_in.shape, F32),
            jax.ShapeDtypeStruct(phases.shape, F32),
            jax.ShapeDtypeStruct(energy.shape, F32),
        ),
        in_specs=[anywhere] + [vmem] * 5 + [smem] * 4 + [anywhere],
        out_specs=(anywhere, vmem, vmem),
        scratch_shapes=[
            pltpu.VMEM((2, members, band, cols), F32),
            pltpu.VMEM((2, members, band, cols), F32),
            pltpu.VMEM(table.shape, BF16),
            pltpu.VMEM((2, 3, SUBLANES, width), F32),
            pltpu.VMEM((2, 2, SUBLANES, width), F32),
            pltpu.VMEM((2, SUBLANES, width), F32),
            pltpu.VMEM((members, 2, SUBLANES, width), F32),
            pltpu.VMEM((2, SUBLANES, width), F32),
            pltpu.VMEM((2, SUBLANES, width), F32),
            pltpu.VMEM((2, 2 * inner, cols), BF16),
            pltpu.VMEM((2, SUBLANES, cols, width), BF16),
            pltpu.VMEM((2 * inner, SUBLANES * width), BF16),
            pltpu.VMEM((groups, SUBLANES, lanes), F32),
            pltpu.VMEM((SUBLANES, lanes), F32),
            dma((members,)), dma((members,)), dma, dma, dma, dma, dma((members,)), dma((members,)),
            dma((members,)), dma((members,)), dma((groups,)), dma((groups,)), dma((4,)),
        ],
        compiler_params=pltpu.CompilerParams(
            collective_id=0, has_side_effects=True, vmem_limit_bytes=40 * 1024 * 1024
        ),
    )(field_in, phases, energy, row_cell, col_cell, weight, charge, pole_rate, pole_freq, pole_amp, table))


def pick_plan(field_in, *others):
    members = field_in.shape[1]
    whole = members == lax.axis_size("trans") and members >= 3 and lax.axis_size("beam") >= 3
    return (whole_slices if whole else shards)(field_in, *others)


def solution(mesh):
    placed = (
        P(None, "beam", "trans", None),
        P("beam", None),
        P("beam", None),
        P("beam", None),
        P("beam", None),
        P("beam", None),
        P("beam"),
        P(),
        P(),
        P(),
    )
    return jax.shard_map(
        pick_plan,
        mesh=mesh,
        in_specs=placed,
        out_specs=(P(None, "beam", "trans", None), P("beam", None), P("beam", None)),
        check_vma=False,
    )
```

```python
import functools
import math

import jax
import jax.numpy as jnp
import ml_dtypes
import numpy as np
from jax import lax
from jax.experimental import pallas as pl
from jax.experimental.pallas import tpu as pltpu
from jax.sharding import PartitionSpec as P

PERIODS = 2


diffraction = 20.0
kick_gain = 0.5
deposit_gain = 0.05
wake_gain = 3.0
charge_unit = 1024.0


def shifted(value, axis, steps):
    count = lax.axis_size(axis)
    first, last = (max(0, -steps), min(count, count - steps))
    return lax.ppermute(value, axis, [(source, source + steps) for source in range(first, last)])


def complex_product(form, left_re, left_im, right_re, right_im):

    def single(first, second):
        return jnp.einsum(form, first, second, precision=lax.Precision.HIGHEST)

    return (
        single(left_re, right_re) - single(left_im, right_im),
        single(left_re, right_im) + single(left_im, right_re),
    )


def dft_table(length, sign):
    counter = jnp.arange(length, dtype=jnp.int32)
    product = counter[:, None] * counter[None, :] % length
    radians = 2.0 * math.pi / length * product.astype(jnp.float32)
    factor = 1.0 / math.sqrt(length)
    return (jnp.cos(radians) * factor, sign * jnp.sin(radians) * factor)


def propagator(row_index, col_index, length):

    def centred(index):
        return ((index + length // 2) % length - length // 2).astype(jnp.float32) / length

    radians = diffraction * (centred(row_index) ** 2 + centred(col_index) ** 2)
    return (jnp.cos(radians), -jnp.sin(radians))


def pole_power(steps, pole_rate, pole_freq):
    damping = jnp.exp(-pole_rate * steps)
    radians = pole_freq * steps
    return (damping * jnp.cos(radians), damping * jnp.sin(radians))


def wake_kicks(charge, pole_rate, pole_freq, pole_amp):
    members = charge.shape[0]
    groups = lax.axis_size("beam")
    position = lax.axis_index("beam")
    charge_norm = charge.astype(jnp.float32) / charge_unit
    offsets = jnp.arange(members, dtype=jnp.float32)
    distance = offsets[:, None] - offsets[None, :]
    inner_re, inner_im = pole_power(jnp.maximum(distance, 0.0)[..., None], pole_rate, pole_freq)
    before = (distance > 0.0)[..., None]
    local_re = jnp.sum(jnp.where(before, inner_re, 0.0) * charge_norm[None, :, None], axis=1)
    tail_re, tail_im = pole_power((members - offsets)[:, None], pole_rate, pole_freq)
    block_re = jnp.sum(charge_norm[:, None] * tail_re, axis=0)
    block_im = jnp.sum(charge_norm[:, None] * tail_im, axis=0)
    gathered_re, gathered_im = (
        lax.all_gather(block_re[None, :], "beam", axis=0, tiled=True),
        lax.all_gather(block_im[None, :], "beam", axis=0, tiled=True),
    )
    sources = jnp.arange(groups, dtype=jnp.int32)
    spacing = (position - 1 - sources).astype(jnp.float32) * members
    reach_re, reach_im = pole_power(jnp.maximum(spacing, 0.0)[:, None], pole_rate, pole_freq)
    valid = (sources < position)[:, None]
    carry_re = jnp.sum(
        jnp.where(valid, gathered_re * reach_re - gathered_im * reach_im, 0.0), axis=0
    )
    carry_im = jnp.sum(
        jnp.where(valid, gathered_re * reach_im + gathered_im * reach_re, 0.0), axis=0
    )
    lead_re, lead_im = pole_power(offsets[:, None], pole_rate, pole_freq)
    state_re = local_re + lead_re * carry_re[None, :] - lead_im * carry_im[None, :]
    summed = jnp.sum(pole_amp[None, :] * (state_re + 0.5 * charge_norm[:, None]), axis=1)
    return wake_gain / (members * groups) * summed


def deposit_slice(band_rows, grid_cols, operands):
    local_row, column, part_re, part_im = operands
    row_hot = (local_row[:, None] == jnp.arange(band_rows, dtype=jnp.int32)[None, :]).astype(
        jnp.bfloat16
    )
    col_hot = (column[:, None] == jnp.arange(grid_cols, dtype=jnp.int32)[None, :]).astype(
        jnp.bfloat16
    )
    spread = jnp.concatenate([col_hot * part_re[:, None], col_hot * part_im[:, None]], axis=1)
    return lax.dot_general(
        row_hot, spread, (((0,), (0,)), ((), ())), preferred_element_type=jnp.float32
    )


def probe_slice(band_rows, grid_cols, operands):
    local_row, column, slab_re, slab_im = operands
    row_hot = (local_row[:, None] == jnp.arange(band_rows, dtype=jnp.int32)[None, :]).astype(
        jnp.float32
    )
    stacked = jnp.concatenate([slab_re, slab_im], axis=1)
    picked = jnp.dot(
        row_hot, stacked, precision=lax.Precision.HIGHEST, preferred_element_type=jnp.float32
    )
    col_hot = column[:, None] == jnp.arange(grid_cols, dtype=jnp.int32)[None, :]
    value_re = jnp.sum(jnp.where(col_hot, picked[:, :grid_cols], 0.0), axis=1)
    value_im = jnp.sum(jnp.where(col_hot, picked[:, grid_cols:], 0.0), axis=1)
    return (value_re, value_im)


def diffract(field_re, field_im, forward, inverse):
    cols_re, cols_im = complex_product("srn,nc->scr", field_re, field_im, forward[0], forward[1])
    halves = lax.all_to_all(
        jnp.stack([cols_re, cols_im]), "trans", split_axis=2, concat_axis=3, tiled=True
    )
    part_re = halves[0]
    part_im = halves[1]
    col_band = part_re.shape[1]
    grid_rows = part_re.shape[2]
    columns = lax.axis_index("trans") * col_band + jnp.arange(col_band, dtype=jnp.int32)
    spec_re, spec_im = complex_product("sqr,rk->sqk", part_re, part_im, forward[0], forward[1])
    kernel_re, kernel_im = propagator(
        jnp.arange(grid_rows, dtype=jnp.int32)[None, :], columns[:, None], grid_rows
    )
    moved_re = spec_re * kernel_re - spec_im * kernel_im
    moved_im = spec_re * kernel_im + spec_im * kernel_re
    back_re, back_im = complex_product("sqk,kr->sqr", moved_re, moved_im, inverse[0], inverse[1])
    rows_both = lax.all_to_all(
        jnp.stack([back_re, back_im]), "trans", split_axis=3, concat_axis=2, tiled=True
    )
    return complex_product("scr,cn->srn", rows_both[0], rows_both[1], inverse[0], inverse[1])


def shards(
    field_in, phases, energy, row_cell, col_cell, weight, charge, pole_rate, pole_freq, pole_amp
):
    field_re = field_in[0]
    field_im = field_in[1]
    slab_count, band_rows, grid_cols = field_re.shape
    row_start = lax.axis_index("trans") * band_rows
    wake_kick = wake_kicks(charge, pole_rate, pole_freq, pole_amp)
    charge_norm = charge.astype(jnp.float32) / charge_unit
    strength = (deposit_gain * charge_norm)[:, None, None]
    local_row = row_cell - row_start
    weights = weight.astype(jnp.float32)
    forward = dft_table(grid_cols, -1.0)
    inverse = dft_table(grid_cols, 1.0)
    depositor = functools.partial(deposit_slice, band_rows, grid_cols)
    reader = functools.partial(probe_slice, band_rows, grid_cols)
    angles = phases
    energies = energy
    for period in range(PERIODS):
        local_re, local_im = lax.map(reader, (local_row, col_cell, field_re, field_im))
        probed = lax.psum(jnp.stack([local_re, local_im]), "trans")
        energies = (
            energies
            - kick_gain * (probed[0] * jnp.cos(angles) - probed[1] * jnp.sin(angles))
            - wake_kick[:, None]
        )
        angles = angles + energies
        part_re = (weights * jnp.cos(angles)).astype(jnp.bfloat16)
        part_im = (-weights * jnp.sin(angles)).astype(jnp.bfloat16)
        bunched = lax.map(depositor, (local_row, col_cell, part_re, part_im))
        field_re = field_re + strength * bunched[:, :, :grid_cols]
        field_im = field_im + strength * bunched[:, :, grid_cols:]
        field_re, field_im = diffract(field_re, field_im, forward, inverse)
        head_slice = shifted(jnp.stack([field_re[-1], field_im[-1]]), "beam", 1)
        field_re = jnp.concatenate([head_slice[0][None], field_re[:-1]], axis=0)
        field_im = jnp.concatenate([head_slice[1][None], field_im[:-1]], axis=0)
    return (jnp.stack([field_re, field_im]), angles, energies)


MESH = pl.DeviceIdType.MESH
LANES = 128
SUBLANES = 8
F32 = jnp.float32
BF16 = jnp.bfloat16


def one_axis_propagator(length):
    index = np.arange(length)
    centred = ((index + length // 2) % length - length // 2) / length
    ring = np.fft.ifft(np.exp(-1j * diffraction * centred**2))
    full = ring[(index[:, None] - index[None, :]) % length]
    block = np.block([[full.real, -full.imag], [full.imag, full.real]]).astype(np.float32)
    upper = block.astype(ml_dtypes.bfloat16)
    lower = (block - upper.astype(np.float32)).astype(ml_dtypes.bfloat16)
    return np.stack([upper, lower])


def two_parts(value):
    upper = value.astype(BF16)
    return upper, (value - upper.astype(F32)).astype(BF16)


def mm(left, right):
    return jnp.dot(left, right, preferred_element_type=F32)


def mm_t(left, right):
    return lax.dot_general(left, right, (((1,), (1,)), ((), ())), preferred_element_type=F32)


def slices_kernel(
    groups,
    field_in, phases_in, energy_in, row_in, col_in, weight_in, charge_in, rate_in, freq_in, amp_in, table,
    field_out, phase_out, energy_out,
    phases, energy, row_cell, col_cell, weight, charge, pole_rate, pole_freq, pole_amp, field, moved, taps, cells, state, result, arrived, probes, parts, halves, col_hot, row_hot, charges, charge_tile,
    field_send, field_recv, cell_send, cell_recv, state_send, state_recv, result_send, result_recv,
    out_send, out_recv, charge_send, charge_recv, local_sems,
):
    beam, trans = lax.axis_index("beam"), lax.axis_index("trans")
    members, band, cols = field_in.shape[1:]
    rows = members * band
    total = groups * members
    half = members // 2
    width = phases.shape[1] // SUBLANES
    edge = rows // 8
    inner = rows - 2 * edge
    mine = beam * members + trans
    ahead, behind = lax.rem(beam + 1, groups), lax.rem(beam + groups - 1, groups)

    barrier = pltpu.get_barrier_semaphore()

    def greet(beam_to, trans_to):
        pl.semaphore_signal(barrier, inc=1, device_id=(beam_to, trans_to), device_id_type=MESH)

    for step in range(1, members):
        greet(beam, lax.rem(trans + step, members))
    for step in range(1, groups):
        greet(lax.rem(beam + step, groups), trans)
    for source in (members - 2, members - 1):
        @pl.when(trans != source)
        def _():
            greet(behind, source)

    @pl.when(trans == members - 1)
    def _():
        greet(ahead, 0)

    small = []
    for k, (source, target) in enumerate((
        (row_in, row_cell), (col_in, col_cell), (weight_in, weight), (phases_in, phases), (energy_in, energy),
        (charge_in, charge), (rate_in, pole_rate), (freq_in, pole_freq), (amp_in, pole_amp),
    )):
        small.append(pltpu.make_async_copy(source, target, local_sems.at[4 + k]))
        small[-1].start()
    take = pltpu.make_async_copy(field_in.at[:, trans], field.at[:, trans], local_sems.at[0])
    take.start()
    take_table = pltpu.make_async_copy(table, taps, local_sems.at[1])
    take_table.start()

    expected = (members - 1) + (groups - 1) + jnp.where(trans >= members - 2, members - 1, 0) + jnp.where(trans == 0, 1, 0)
    pl.semaphore_wait(barrier, expected)

    def remote(source, target, send, recv, beam_to, trans_to):
        return pltpu.make_async_remote_copy(
            src_ref=source, dst_ref=target, send_sem=send, recv_sem=recv,
            device_id=(beam_to, trans_to), device_id_type=MESH,
        )

    field_copies = []
    way = jnp.where(trans < half, 1, members - 1)
    for step in [half] + [k for k in range(1, members) if k != half]:
        to = lax.rem(trans + way * step, members)
        copy = remote(field_in.at[:, to], field.at[:, trans], field_send.at[step], field_recv.at[trans], beam, to)
        copy.start()
        field_copies.append(copy)

    for copy in small:
        copy.wait()

    lane = lax.broadcasted_iota(jnp.int32, charge_tile.shape, 1)
    own = jnp.zeros(charge_tile.shape, F32)
    for k in range(members):
        own = jnp.where(lane == beam * members + k, charge[k].astype(F32) / charge_unit, own)
    charge_tile[...] = own
    charges[pl.ds(beam, 1)] = own[None]
    charge_copies = []
    for step in range(1, groups):
        copy = remote(charge_tile, charges.at[beam], charge_send.at[step], charge_recv.at[beam], lax.rem(beam + step, groups), trans)
        copy.start()
        charge_copies.append(copy)

    for k in range(SUBLANES):
        here = pl.ds(k * width, width)
        for place, source in enumerate((row_cell, col_cell, weight)):
            cells[0, place, k : k + 1, :] = source[pl.ds(trans, 1), here].astype(F32)
        state[0, 0, k : k + 1, :] = phases[pl.ds(trans, 1), here]
        state[0, 1, k : k + 1, :] = energy[pl.ds(trans, 1), here]
    first = trans == 0
    prior_beam = jnp.where(first, behind, beam)
    prior_trans = jnp.where(first, members - 1, trans - 1)
    cell_copy = remote(cells.at[0], cells.at[1], cell_send, cell_recv, prior_beam, prior_trans)
    cell_copy.start()

    def one_hots(period):
        col_index = lax.broadcasted_iota(jnp.int32, (cols, width), 0).astype(F32)

        def body(k, carry):
            col_hot[period, k] = jnp.where(cells[period, 1, pl.ds(k, 1), :] == col_index, 1.0, 0.0).astype(BF16)
            return carry

        lax.fori_loop(0, SUBLANES, body, 0)

    one_hots(0)

    for step in range(1, groups):
        source = lax.rem(beam + step, groups)
        remote(charge_tile, charges.at[source], charge_send.at[step], charge_recv.at[source], source, trans).wait_recv()
    every = jnp.sum(charges[...], axis=0)

    def wake_and_charge(slice_id):
        distance = slice_id - lane
        ago = jnp.maximum(distance, 0).astype(F32)
        memory = jnp.zeros(lane.shape, F32)
        amount = F32(0)
        for k in range(pole_rate.shape[0]):
            memory = memory + pole_amp[k] * (jnp.exp(-pole_rate[k] * ago) * jnp.cos(pole_freq[k] * ago))
            amount = amount + pole_amp[k]
        memory = jnp.where(distance > 0, memory, jnp.where(distance == 0, 0.5 * amount, 0.0))
        wake = (wake_gain / total) * jnp.sum(memory * every, axis=1, keepdims=True)
        return wake, jnp.sum(jnp.where(distance == 0, every, 0.0), axis=1, keepdims=True)

    following = lax.rem(mine + 1, total)
    wakes = [wake_and_charge(mine), wake_and_charge(following)]
    cell_copy.wait_recv()
    one_hots(1)
    start_cos, start_sin = jnp.cos(state[0, 0]), jnp.sin(state[0, 0])

    row_index = lax.broadcasted_iota(jnp.int32, (inner, width), 0).astype(F32) + float(edge)

    def probe_band(source, opens):
        upper, lower = two_parts(field[:, source].reshape(2 * band, cols))
        band_index = (lax.broadcasted_iota(jnp.int32, (band, width), 0) + source * band).astype(F32)

        def body(k, carry):
            hot = col_hot[0, k]
            picked = mm(upper, hot) + mm(lower, hot)
            inside = cells[0, 0, pl.ds(k, 1), :] == band_index
            for part in range(2):
                found = jnp.sum(
                    jnp.where(inside, picked[part * band : (part + 1) * band], 0.0), axis=0, keepdims=True
                )
                probes[part, pl.ds(k, 1), :] = found if opens else probes[part, pl.ds(k, 1), :] + found
            return carry

        lax.fori_loop(0, SUBLANES, body, 0, unroll=True)

    def probe(period):
        flat = field[...].reshape(2, rows, cols)
        for part in range(2):
            upper, lower = two_parts(flat[part, edge : rows - edge])
            halves[0, part * inner : (part + 1) * inner, :] = upper
            halves[1, part * inner : (part + 1) * inner, :] = lower

        def body(k, carry):
            hot = col_hot[period, k]
            picked = mm(halves[0], hot) + mm(halves[1], hot)
            inside = cells[period, 0, pl.ds(k, 1), :] == row_index
            probes[0, pl.ds(k, 1), :] = jnp.sum(jnp.where(inside, picked[:inner], 0.0), axis=0, keepdims=True)
            probes[1, pl.ds(k, 1), :] = jnp.sum(jnp.where(inside, picked[inner:], 0.0), axis=0, keepdims=True)
            return carry

        lax.fori_loop(0, SUBLANES, body, 0, unroll=True)

    def push(period, cos_now, sin_now):
        eta = state[period, 1] - kick_gain * (probes[0] * cos_now - probes[1] * sin_now) - wakes[period][0]
        theta = state[period, 0] + eta
        return theta, eta

    def deposit(period, theta):
        heavy = cells[period, 2]
        parts[0] = (heavy * jnp.cos(theta)).astype(BF16).astype(F32)
        parts[1] = (-heavy * jnp.sin(theta)).astype(BF16).astype(F32)
        bunched = jnp.zeros((2 * inner, cols), F32)
        for k in range(SUBLANES):
            inside = cells[period, 0, k : k + 1, :] == row_index
            spread = jnp.concatenate(
                [jnp.where(inside, parts[part, k : k + 1, :], 0.0).astype(BF16) for part in range(2)], axis=0
            )
            row_hot[:, k * width : (k + 1) * width] = spread
            bunched = bunched + mm_t(row_hot[:, k * width : (k + 1) * width], col_hot[period, k])
        strength = deposit_gain * wakes[period][1][:1, :1]
        flat = field[...].reshape(2, rows, cols)
        wide = []
        for part in range(2):
            loaded = flat[part, edge : rows - edge] + strength * bunched[part * inner : (part + 1) * inner]
            wide.append(jnp.concatenate([flat[part, :edge], loaded, flat[part, rows - edge :]], axis=0))
        upper, lower = two_parts(jnp.concatenate(wide, axis=1))
        across = mm_t(upper, taps[0]) + (mm_t(lower, taps[0]) + mm_t(upper, taps[1]))
        return two_parts(jnp.concatenate([across[:, :cols], across[:, cols:]], axis=0))

    def along_rows(first_row, count, upper, lower):
        here = [pl.ds(pl.multiple_of(part * rows + first_row, band), count) for part in range(2)]
        major, minor = (jnp.concatenate([taps[part, where] for where in here], axis=0) for part in range(2))
        return (mm(major, upper) + (mm(major, lower) + mm(minor, upper))).reshape(2, count, cols)

    take.wait()
    probe_band(trans, True)
    for step in range(1, members):
        source = lax.rem(trans + way * step, members)
        remote(field_in.at[:, source], field.at[:, source], field_send.at[step], field_recv.at[source], beam, source).wait_recv()
        probe_band(source, False)
    take_table.wait()
    theta, eta = push(0, start_cos, start_sin)
    state[0, 0] = theta
    state[0, 1] = eta
    state_copy = remote(state.at[0], state.at[1], state_send, state_recv, prior_beam, prior_trans)
    state_copy.start()
    turned = along_rows(0, rows, *deposit(0, theta))
    field[...] = jnp.where(following == 0, 0.0, turned).reshape(field.shape)

    state_copy.wait_recv()
    probe(1)
    theta, eta = push(1, jnp.cos(state[1, 0]), jnp.sin(state[1, 0]))
    result[0] = theta
    result[1] = eta

    def scatter(shift, source_of, target, send, recv, sem):
        slot = lax.rem(trans + shift, members)
        stays = trans + shift < members
        beam_to = jnp.where(stays, beam, ahead)

        def away(to):
            return remote(source_of(to), target(slot), send.at[to], recv.at[slot], beam_to, to)

        def here():
            return pltpu.make_async_copy(source_of(trans), target(slot), sem)

        def start(to):
            same = jnp.logical_and(stays, to == trans)

            @pl.when(same)
            def _():
                here().start()

            @pl.when(jnp.logical_not(same))
            def _():
                away(to).start()

        def finish():
            for to in range(members):
                @pl.when(jnp.logical_not(jnp.logical_and(stays, to == trans)))
                def _():
                    away(to).wait_send()

            @pl.when(stays)
            def _():
                here().wait()

            for place in range(members):
                def wait_for():
                    remote(source_of(trans), target(place), send.at[0], recv.at[place], beam, trans).wait_recv()

                if place < shift:
                    wait_for()
                else:
                    pl.when(trans != place - shift)(wait_for)

        return start, finish

    start_result, finish_result = scatter(
        1, lambda to: result, lambda slot: arrived.at[slot], result_send, result_recv, local_sems.at[2]
    )
    for to in range(members):
        start_result(to)
    upper, lower = deposit(1, theta)
    start_field, finish_field = scatter(
        2, lambda to: moved.at[:, to], lambda slot: field_out.at[:, slot], out_send, out_recv, local_sems.at[3]
    )
    mine_half = trans // half
    for side in (1 - mine_half, mine_half):
        turned = along_rows(side * (half * band), half * band, upper, lower)
        turned = jnp.where(lax.rem(mine + 2, total) == 0, 0.0, turned)
        for k in range(half):
            moved[:, side * half + k] = turned[:, k * band : (k + 1) * band]
            start_field(side * half + k)

    finish_result()
    for place in range(members):
        for k in range(SUBLANES):
            here = slice(k * width, (k + 1) * width)
            phase_out[place : place + 1, here] = arrived[place, 0, k : k + 1, :]
            energy_out[place : place + 1, here] = arrived[place, 1, k : k + 1, :]
    for copy in field_copies + charge_copies + [cell_copy, state_copy]:
        copy.wait_send()
    finish_field()


def whole_slices(
    field_in, phases, energy, row_cell, col_cell, weight, charge, pole_rate, pole_freq, pole_amp
):
    groups, members = lax.axis_size("beam"), lax.axis_size("trans")
    band, cols = field_in.shape[2:]
    rows = members * band
    inner = rows - 2 * (rows // 8)
    width = phases.shape[1] // SUBLANES
    lanes = -(-groups * members // LANES) * LANES
    table = jnp.asarray(one_axis_propagator(cols))
    vmem, hbm = (pl.BlockSpec(memory_space=space) for space in (pltpu.VMEM, pltpu.HBM))
    dma = pltpu.SemaphoreType.DMA
    return tuple(pl.pallas_call(
        functools.partial(slices_kernel, groups),
        out_shape=(
            jax.ShapeDtypeStruct(field_in.shape, F32),
            jax.ShapeDtypeStruct(phases.shape, F32),
            jax.ShapeDtypeStruct(energy.shape, F32),
        ),
        in_specs=[hbm] * 11,
        out_specs=(hbm, vmem, vmem),
        scratch_shapes=[
            *[pltpu.VMEM(array.shape, array.dtype) for array in (phases, energy, row_cell, col_cell, weight)],
            *[pltpu.SMEM(array.shape, array.dtype) for array in (charge, pole_rate, pole_freq, pole_amp)],
            pltpu.VMEM((2, members, band, cols), F32),
            pltpu.VMEM((2, members, band, cols), F32),
            pltpu.VMEM(table.shape, BF16),
            pltpu.VMEM((2, 3, SUBLANES, width), F32),
            pltpu.VMEM((2, 2, SUBLANES, width), F32),
            pltpu.VMEM((2, SUBLANES, width), F32),
            pltpu.VMEM((members, 2, SUBLANES, width), F32),
            pltpu.VMEM((2, SUBLANES, width), F32),
            pltpu.VMEM((2, SUBLANES, width), F32),
            pltpu.VMEM((2, 2 * inner, cols), BF16),
            pltpu.VMEM((2, SUBLANES, cols, width), BF16),
            pltpu.VMEM((2 * inner, SUBLANES * width), BF16),
            pltpu.VMEM((groups, SUBLANES, lanes), F32),
            pltpu.VMEM((SUBLANES, lanes), F32),
            dma((members,)), dma((members,)), dma, dma, dma, dma, dma((members,)), dma((members,)),
            dma((members,)), dma((members,)), dma((groups,)), dma((groups,)), dma((13,)),
        ],
        compiler_params=pltpu.CompilerParams(
            collective_id=0, has_side_effects=True, vmem_limit_bytes=64 * 1024 * 1024 - 64 * 1024
        ),
    )(field_in, phases, energy, row_cell, col_cell, weight, charge, pole_rate, pole_freq, pole_amp, table))


def pick_plan(field_in, *others):
    members = field_in.shape[1]
    whole = members == lax.axis_size("trans") and members % 2 == 0 and members >= 4 and lax.axis_size("beam") >= 3
    return (whole_slices if whole else shards)(field_in, *others)


def solution(mesh):
    placed = (
        P(None, "beam", "trans", None),
        P("beam", None),
        P("beam", None),
        P("beam", None),
        P("beam", None),
        P("beam", None),
        P("beam"),
        P(),
        P(),
        P(),
    )
    return jax.shard_map(
        pick_plan,
        mesh=mesh,
        in_specs=placed,
        out_specs=(P(None, "beam", "trans", None), P("beam", None), P("beam", None)),
        check_vma=False,
    )
```

```python
import functools
import math

import jax
import jax.numpy as jnp
import ml_dtypes
import numpy as np
from jax import lax
from jax.experimental import pallas as pl
from jax.experimental.pallas import tpu as pltpu
from jax.sharding import PartitionSpec as P

PERIODS = 2


diffraction = 20.0
kick_gain = 0.5
deposit_gain = 0.05
wake_gain = 3.0
charge_unit = 1024.0


def shifted(value, axis, steps):
    count = lax.axis_size(axis)
    first, last = (max(0, -steps), min(count, count - steps))
    return lax.ppermute(value, axis, [(source, source + steps) for source in range(first, last)])


def complex_product(form, left_re, left_im, right_re, right_im):

    def single(first, second):
        return jnp.einsum(form, first, second, precision=lax.Precision.HIGHEST)

    return (
        single(left_re, right_re) - single(left_im, right_im),
        single(left_re, right_im) + single(left_im, right_re),
    )


def dft_table(length, sign):
    counter = jnp.arange(length, dtype=jnp.int32)
    product = counter[:, None] * counter[None, :] % length
    radians = 2.0 * math.pi / length * product.astype(jnp.float32)
    factor = 1.0 / math.sqrt(length)
    return (jnp.cos(radians) * factor, sign * jnp.sin(radians) * factor)


def propagator(row_index, col_index, length):

    def centred(index):
        return ((index + length // 2) % length - length // 2).astype(jnp.float32) / length

    radians = diffraction * (centred(row_index) ** 2 + centred(col_index) ** 2)
    return (jnp.cos(radians), -jnp.sin(radians))


def pole_power(steps, pole_rate, pole_freq):
    damping = jnp.exp(-pole_rate * steps)
    radians = pole_freq * steps
    return (damping * jnp.cos(radians), damping * jnp.sin(radians))


def wake_kicks(charge, pole_rate, pole_freq, pole_amp):
    members = charge.shape[0]
    groups = lax.axis_size("beam")
    position = lax.axis_index("beam")
    charge_norm = charge.astype(jnp.float32) / charge_unit
    offsets = jnp.arange(members, dtype=jnp.float32)
    distance = offsets[:, None] - offsets[None, :]
    inner_re, inner_im = pole_power(jnp.maximum(distance, 0.0)[..., None], pole_rate, pole_freq)
    before = (distance > 0.0)[..., None]
    local_re = jnp.sum(jnp.where(before, inner_re, 0.0) * charge_norm[None, :, None], axis=1)
    tail_re, tail_im = pole_power((members - offsets)[:, None], pole_rate, pole_freq)
    block_re = jnp.sum(charge_norm[:, None] * tail_re, axis=0)
    block_im = jnp.sum(charge_norm[:, None] * tail_im, axis=0)
    gathered_re, gathered_im = (
        lax.all_gather(block_re[None, :], "beam", axis=0, tiled=True),
        lax.all_gather(block_im[None, :], "beam", axis=0, tiled=True),
    )
    sources = jnp.arange(groups, dtype=jnp.int32)
    spacing = (position - 1 - sources).astype(jnp.float32) * members
    reach_re, reach_im = pole_power(jnp.maximum(spacing, 0.0)[:, None], pole_rate, pole_freq)
    valid = (sources < position)[:, None]
    carry_re = jnp.sum(
        jnp.where(valid, gathered_re * reach_re - gathered_im * reach_im, 0.0), axis=0
    )
    carry_im = jnp.sum(
        jnp.where(valid, gathered_re * reach_im + gathered_im * reach_re, 0.0), axis=0
    )
    lead_re, lead_im = pole_power(offsets[:, None], pole_rate, pole_freq)
    state_re = local_re + lead_re * carry_re[None, :] - lead_im * carry_im[None, :]
    summed = jnp.sum(pole_amp[None, :] * (state_re + 0.5 * charge_norm[:, None]), axis=1)
    return wake_gain / (members * groups) * summed


def deposit_slice(band_rows, grid_cols, operands):
    local_row, column, part_re, part_im = operands
    row_hot = (local_row[:, None] == jnp.arange(band_rows, dtype=jnp.int32)[None, :]).astype(
        jnp.bfloat16
    )
    col_hot = (column[:, None] == jnp.arange(grid_cols, dtype=jnp.int32)[None, :]).astype(
        jnp.bfloat16
    )
    spread = jnp.concatenate([col_hot * part_re[:, None], col_hot * part_im[:, None]], axis=1)
    return lax.dot_general(
        row_hot, spread, (((0,), (0,)), ((), ())), preferred_element_type=jnp.float32
    )


def probe_slice(band_rows, grid_cols, operands):
    local_row, column, slab_re, slab_im = operands
    row_hot = (local_row[:, None] == jnp.arange(band_rows, dtype=jnp.int32)[None, :]).astype(
        jnp.float32
    )
    stacked = jnp.concatenate([slab_re, slab_im], axis=1)
    picked = jnp.dot(
        row_hot, stacked, precision=lax.Precision.HIGHEST, preferred_element_type=jnp.float32
    )
    col_hot = column[:, None] == jnp.arange(grid_cols, dtype=jnp.int32)[None, :]
    value_re = jnp.sum(jnp.where(col_hot, picked[:, :grid_cols], 0.0), axis=1)
    value_im = jnp.sum(jnp.where(col_hot, picked[:, grid_cols:], 0.0), axis=1)
    return (value_re, value_im)


def diffract(field_re, field_im, forward, inverse):
    cols_re, cols_im = complex_product("srn,nc->scr", field_re, field_im, forward[0], forward[1])
    halves = lax.all_to_all(
        jnp.stack([cols_re, cols_im]), "trans", split_axis=2, concat_axis=3, tiled=True
    )
    part_re = halves[0]
    part_im = halves[1]
    col_band = part_re.shape[1]
    grid_rows = part_re.shape[2]
    columns = lax.axis_index("trans") * col_band + jnp.arange(col_band, dtype=jnp.int32)
    spec_re, spec_im = complex_product("sqr,rk->sqk", part_re, part_im, forward[0], forward[1])
    kernel_re, kernel_im = propagator(
        jnp.arange(grid_rows, dtype=jnp.int32)[None, :], columns[:, None], grid_rows
    )
    moved_re = spec_re * kernel_re - spec_im * kernel_im
    moved_im = spec_re * kernel_im + spec_im * kernel_re
    back_re, back_im = complex_product("sqk,kr->sqr", moved_re, moved_im, inverse[0], inverse[1])
    rows_both = lax.all_to_all(
        jnp.stack([back_re, back_im]), "trans", split_axis=3, concat_axis=2, tiled=True
    )
    return complex_product("scr,cn->srn", rows_both[0], rows_both[1], inverse[0], inverse[1])


def shards(
    field_in, phases, energy, row_cell, col_cell, weight, charge, pole_rate, pole_freq, pole_amp
):
    field_re = field_in[0]
    field_im = field_in[1]
    slab_count, band_rows, grid_cols = field_re.shape
    row_start = lax.axis_index("trans") * band_rows
    wake_kick = wake_kicks(charge, pole_rate, pole_freq, pole_amp)
    charge_norm = charge.astype(jnp.float32) / charge_unit
    strength = (deposit_gain * charge_norm)[:, None, None]
    local_row = row_cell - row_start
    weights = weight.astype(jnp.float32)
    forward = dft_table(grid_cols, -1.0)
    inverse = dft_table(grid_cols, 1.0)
    depositor = functools.partial(deposit_slice, band_rows, grid_cols)
    reader = functools.partial(probe_slice, band_rows, grid_cols)
    angles = phases
    energies = energy
    for period in range(PERIODS):
        local_re, local_im = lax.map(reader, (local_row, col_cell, field_re, field_im))
        probed = lax.psum(jnp.stack([local_re, local_im]), "trans")
        energies = (
            energies
            - kick_gain * (probed[0] * jnp.cos(angles) - probed[1] * jnp.sin(angles))
            - wake_kick[:, None]
        )
        angles = angles + energies
        part_re = (weights * jnp.cos(angles)).astype(jnp.bfloat16)
        part_im = (-weights * jnp.sin(angles)).astype(jnp.bfloat16)
        bunched = lax.map(depositor, (local_row, col_cell, part_re, part_im))
        field_re = field_re + strength * bunched[:, :, :grid_cols]
        field_im = field_im + strength * bunched[:, :, grid_cols:]
        field_re, field_im = diffract(field_re, field_im, forward, inverse)
        head_slice = shifted(jnp.stack([field_re[-1], field_im[-1]]), "beam", 1)
        field_re = jnp.concatenate([head_slice[0][None], field_re[:-1]], axis=0)
        field_im = jnp.concatenate([head_slice[1][None], field_im[:-1]], axis=0)
    return (jnp.stack([field_re, field_im]), angles, energies)


MESH = pl.DeviceIdType.MESH
LANES = 128
SUBLANES = 8
VMEM_GRANT = 64 * 1024 * 1024 - 64 * 1024
F32 = jnp.float32
BF16 = jnp.bfloat16


def one_axis_propagator(length):
    index = np.arange(length)
    centred = ((index + length // 2) % length - length // 2) / length
    ring = np.fft.ifft(np.exp(-1j * diffraction * centred**2))
    full = ring[(index[:, None] - index[None, :]) % length]
    block = np.block([[full.real, -full.imag], [full.imag, full.real]]).astype(np.float32)
    upper = block.astype(ml_dtypes.bfloat16)
    lower = (block - upper.astype(np.float32)).astype(ml_dtypes.bfloat16)
    return np.stack([upper, lower])


def two_parts(value):
    upper = value.astype(BF16)
    return upper, (value - upper.astype(F32)).astype(BF16)


def mm(left, right):
    return jnp.dot(left, right, preferred_element_type=F32)


def slices_kernel(
    groups,
    field_in, phases_in, energy_in, row_in, col_in, weight_in, charge_in, rate_in, freq_in, amp_in, table,
    field_out, phase_out, energy_out,
    phases, energy, row_cell, col_cell, weight, charge, pole_rate, pole_freq, pole_amp, field, moved, taps, cells, state, result, arrived, probes, parts, halves, col_hot, col_hot_t, taps_t, row_hot, charges, charge_tile,
    field_send, field_recv, cell_send, cell_recv, state_send, state_recv, result_send, result_recv,
    out_send, out_recv, charge_send, charge_recv, local_sems,
):
    beam, trans = lax.axis_index("beam"), lax.axis_index("trans")
    members, band, cols = field_in.shape[1:]
    rows = members * band
    total = groups * members
    half = members // 2
    width = phases.shape[1] // SUBLANES
    edge = rows // 8
    inner = rows - 2 * edge
    mine = beam * members + trans
    ahead, behind = lax.rem(beam + 1, groups), lax.rem(beam + groups - 1, groups)

    barrier = pltpu.get_barrier_semaphore()

    def greet(beam_to, trans_to):
        pl.semaphore_signal(barrier, inc=1, device_id=(beam_to, trans_to), device_id_type=MESH)

    for step in range(1, members):
        greet(beam, lax.rem(trans + step, members))
    for step in range(1, groups):
        greet(lax.rem(beam + step, groups), trans)
    for source in (members - 2, members - 1):
        @pl.when(trans != source)
        def _():
            greet(behind, source)

    @pl.when(trans == members - 1)
    def _():
        greet(ahead, 0)

    small = []
    for k, (source, target) in enumerate((
        (row_in, row_cell), (col_in, col_cell), (weight_in, weight), (phases_in, phases), (energy_in, energy),
        (charge_in, charge), (rate_in, pole_rate), (freq_in, pole_freq), (amp_in, pole_amp),
    )):
        small.append(pltpu.make_async_copy(source, target, local_sems.at[4 + k]))
        small[-1].start()
    take = pltpu.make_async_copy(field_in.at[:, trans], field.at[:, trans], local_sems.at[0])
    take.start()
    take_table = pltpu.make_async_copy(table, taps, local_sems.at[1])
    take_table.start()

    expected = (members - 1) + (groups - 1) + jnp.where(trans >= members - 2, members - 1, 0) + jnp.where(trans == 0, 1, 0)
    pl.semaphore_wait(barrier, expected)

    def remote(source, target, send, recv, beam_to, trans_to):
        return pltpu.make_async_remote_copy(
            src_ref=source, dst_ref=target, send_sem=send, recv_sem=recv,
            device_id=(beam_to, trans_to), device_id_type=MESH,
        )

    field_copies = []
    way = jnp.where(trans < half, 1, members - 1)
    mine_half = trans // half
    beyond = [(1 - mine_half) * half + lax.rem(trans + k, half) for k in range(half)]
    nearby = [mine_half * half + lax.rem(trans + k, half) for k in range(1, half)]
    for to in beyond + nearby:
        copy = remote(field_in.at[:, to], field.at[:, trans], field_send.at[to], field_recv.at[trans], beam, to)
        copy.start()
        field_copies.append(copy)

    for copy in small:
        copy.wait()

    lane = lax.broadcasted_iota(jnp.int32, charge_tile.shape, 1)
    own = jnp.zeros(charge_tile.shape, F32)
    for k in range(members):
        own = jnp.where(lane == beam * members + k, charge[k].astype(F32) / charge_unit, own)
    charge_tile[...] = own
    charges[pl.ds(beam, 1)] = own[None]
    charge_copies = []
    for step in range(1, groups):
        copy = remote(charge_tile, charges.at[beam], charge_send.at[step], charge_recv.at[beam], lax.rem(beam + step, groups), trans)
        copy.start()
        charge_copies.append(copy)

    for k in range(SUBLANES):
        here = pl.ds(k * width, width)
        for place, source in enumerate((row_cell, col_cell, weight)):
            cells[0, place, k : k + 1, :] = source[pl.ds(trans, 1), here].astype(F32)
        state[0, 0, k : k + 1, :] = phases[pl.ds(trans, 1), here]
        state[0, 1, k : k + 1, :] = energy[pl.ds(trans, 1), here]
    first = trans == 0
    prior_beam = jnp.where(first, behind, beam)
    prior_trans = jnp.where(first, members - 1, trans - 1)
    cell_copy = remote(cells.at[0], cells.at[1], cell_send, cell_recv, prior_beam, prior_trans)
    cell_copy.start()

    def one_hots(period):
        col_index = lax.broadcasted_iota(jnp.int32, (cols, width), 0).astype(F32)

        def body(k, carry):
            hot = jnp.where(cells[period, 1, pl.ds(k, 1), :] == col_index, 1.0, 0.0)
            col_hot[period, k] = hot.astype(BF16)
            col_hot_t[period, k] = hot.T.astype(BF16)
            return carry

        lax.fori_loop(0, SUBLANES, body, 0)

    one_hots(0)

    for step in range(1, groups):
        source = lax.rem(beam + step, groups)
        remote(charge_tile, charges.at[source], charge_send.at[step], charge_recv.at[source], source, trans).wait_recv()
    every = jnp.sum(charges[...], axis=0)

    def wake_and_charge(slice_id):
        distance = slice_id - lane
        ago = jnp.maximum(distance, 0).astype(F32)
        memory = jnp.zeros(lane.shape, F32)
        amount = F32(0)
        for k in range(pole_rate.shape[0]):
            memory = memory + pole_amp[k] * (jnp.exp(-pole_rate[k] * ago) * jnp.cos(pole_freq[k] * ago))
            amount = amount + pole_amp[k]
        memory = jnp.where(distance > 0, memory, jnp.where(distance == 0, 0.5 * amount, 0.0))
        wake = (wake_gain / total) * jnp.sum(memory * every, axis=1, keepdims=True)
        return wake, jnp.sum(jnp.where(distance == 0, every, 0.0), axis=1, keepdims=True)

    following = lax.rem(mine + 1, total)
    wakes = [wake_and_charge(mine), wake_and_charge(following)]
    cell_copy.wait_recv()
    one_hots(1)
    start_cos, start_sin = jnp.cos(state[0, 0]), jnp.sin(state[0, 0])

    row_index = lax.broadcasted_iota(jnp.int32, (inner, width), 0).astype(F32) + float(edge)

    def probe_band(source, opens):
        upper, lower = two_parts(field[:, source].reshape(2 * band, cols))
        band_index = (lax.broadcasted_iota(jnp.int32, (band, width), 0) + source * band).astype(F32)

        def body(k, carry):
            hot = col_hot[0, k]
            picked = mm(upper, hot) + mm(lower, hot)
            inside = cells[0, 0, pl.ds(k, 1), :] == band_index
            for part in range(2):
                found = jnp.sum(
                    jnp.where(inside, picked[part * band : (part + 1) * band], 0.0), axis=0, keepdims=True
                )
                probes[part, pl.ds(k, 1), :] = found if opens else probes[part, pl.ds(k, 1), :] + found
            return carry

        lax.fori_loop(0, SUBLANES, body, 0, unroll=True)

    def probe(period):
        flat = field[...].reshape(2, rows, cols)
        for part in range(2):
            upper, lower = two_parts(flat[part, edge : rows - edge])
            halves[0, part * inner : (part + 1) * inner, :] = upper
            halves[1, part * inner : (part + 1) * inner, :] = lower

        def body(k, carry):
            hot = col_hot[period, k]
            picked = mm(halves[0], hot) + mm(halves[1], hot)
            inside = cells[period, 0, pl.ds(k, 1), :] == row_index
            probes[0, pl.ds(k, 1), :] = jnp.sum(jnp.where(inside, picked[:inner], 0.0), axis=0, keepdims=True)
            probes[1, pl.ds(k, 1), :] = jnp.sum(jnp.where(inside, picked[inner:], 0.0), axis=0, keepdims=True)
            return carry

        lax.fori_loop(0, SUBLANES, body, 0, unroll=True)

    def push(period, cos_now, sin_now):
        eta = state[period, 1] - kick_gain * (probes[0] * cos_now - probes[1] * sin_now) - wakes[period][0]
        theta = state[period, 0] + eta
        return theta, eta

    def deposit(period, theta):
        heavy = cells[period, 2]
        parts[0] = (heavy * jnp.cos(theta)).astype(BF16).astype(F32)
        parts[1] = (-heavy * jnp.sin(theta)).astype(BF16).astype(F32)
        bunched = jnp.zeros((2 * inner, cols), F32)
        for k in range(SUBLANES):
            inside = cells[period, 0, k : k + 1, :] == row_index
            spread = jnp.concatenate(
                [jnp.where(inside, parts[part, k : k + 1, :], 0.0).astype(BF16) for part in range(2)], axis=0
            )
            row_hot[:, k * width : (k + 1) * width] = spread
            bunched = bunched + mm(row_hot[:, k * width : (k + 1) * width], col_hot_t[period, k])
        strength = deposit_gain * wakes[period][1][:1, :1]
        flat = field[...].reshape(2, rows, cols)
        wide = []
        for part in range(2):
            loaded = flat[part, edge : rows - edge] + strength * bunched[part * inner : (part + 1) * inner]
            wide.append(jnp.concatenate([flat[part, :edge], loaded, flat[part, rows - edge :]], axis=0))
        upper, lower = two_parts(jnp.concatenate(wide, axis=1))
        across = mm(upper, taps_t[0]) + (mm(lower, taps_t[0]) + mm(upper, taps_t[1]))
        return two_parts(jnp.concatenate([across[:, :cols], across[:, cols:]], axis=0))

    def along_rows(first_row, count, upper, lower):
        here = [pl.ds(pl.multiple_of(part * rows + first_row, band), count) for part in range(2)]
        major, minor = (jnp.concatenate([taps[part, where] for where in here], axis=0) for part in range(2))
        return (mm(major, upper) + (mm(major, lower) + mm(minor, upper))).reshape(2, count, cols)

    take_table.wait()
    for part in range(2):
        both = taps[part]
        taps_t[part, :cols] = jnp.concatenate([both[:cols, :cols], both[cols:, :cols]], axis=1)
        taps_t[part, cols:] = jnp.concatenate([both[:cols, cols:], both[cols:, cols:]], axis=1)
    take.wait()
    probe_band(trans, True)
    for step in range(1, members):
        source = lax.rem(trans + way * step, members)
        remote(field_in.at[:, source], field.at[:, source], field_send.at[source], field_recv.at[source], beam, source).wait_recv()
        probe_band(source, False)
    theta, eta = push(0, start_cos, start_sin)
    state[0, 0] = theta
    state[0, 1] = eta
    state_copy = remote(state.at[0], state.at[1], state_send, state_recv, prior_beam, prior_trans)
    state_copy.start()
    turned = along_rows(0, rows, *deposit(0, theta))
    field[...] = jnp.where(following == 0, 0.0, turned).reshape(field.shape)

    state_copy.wait_recv()
    probe(1)
    theta, eta = push(1, jnp.cos(state[1, 0]), jnp.sin(state[1, 0]))
    result[0] = theta
    result[1] = eta

    def scatter(shift, source_of, target, send, recv, sem):
        slot = lax.rem(trans + shift, members)
        stays = trans + shift < members
        beam_to = jnp.where(stays, beam, ahead)

        def away(to):
            return remote(source_of(to), target(slot), send.at[to], recv.at[slot], beam_to, to)

        def here():
            return pltpu.make_async_copy(source_of(trans), target(slot), sem)

        def start(to):
            same = jnp.logical_and(stays, to == trans)

            @pl.when(same)
            def _():
                here().start()

            @pl.when(jnp.logical_not(same))
            def _():
                away(to).start()

        def finish():
            for to in range(members):
                @pl.when(jnp.logical_not(jnp.logical_and(stays, to == trans)))
                def _():
                    away(to).wait_send()

            @pl.when(stays)
            def _():
                here().wait()

            for place in range(members):
                def wait_for():
                    remote(source_of(trans), target(place), send.at[0], recv.at[place], beam, trans).wait_recv()

                if place < shift:
                    wait_for()
                else:
                    pl.when(trans != place - shift)(wait_for)

        return start, finish

    start_result, finish_result = scatter(
        1, lambda to: result, lambda slot: arrived.at[slot], result_send, result_recv, local_sems.at[2]
    )
    for to in range(members):
        start_result(to)
    upper, lower = deposit(1, theta)
    start_field, finish_field = scatter(
        2, lambda to: moved.at[:, to], lambda slot: field_out.at[:, slot], out_send, out_recv, local_sems.at[3]
    )
    for side in (1 - mine_half, mine_half):
        turned = along_rows(side * (half * band), half * band, upper, lower)
        turned = jnp.where(lax.rem(mine + 2, total) == 0, 0.0, turned)
        for k in range(half):
            moved[:, side * half + k] = turned[:, k * band : (k + 1) * band]
            start_field(side * half + k)

    finish_result()
    for place in range(members):
        for k in range(SUBLANES):
            here = slice(k * width, (k + 1) * width)
            phase_out[place : place + 1, here] = arrived[place, 0, k : k + 1, :]
            energy_out[place : place + 1, here] = arrived[place, 1, k : k + 1, :]
    for copy in field_copies + charge_copies + [cell_copy, state_copy]:
        copy.wait_send()
    finish_field()


def settle_kernel(field_made, phase_made, energy_made, field_out, phase_out, energy_out, sems):
    pieces = [(phase_made, phase_out), (energy_made, energy_out)]
    for part in range(2):
        for place in range(field_made.shape[1]):
            pieces.append((field_made.at[part, place], field_out.at[part, place]))
    copies = [pltpu.make_async_copy(*piece, sems.at[k]) for k, piece in enumerate(pieces)]
    for copy in copies:
        copy.start()
    for copy in copies:
        copy.wait()


def whole_slices(
    field_in, phases, energy, row_cell, col_cell, weight, charge, pole_rate, pole_freq, pole_amp
):
    groups, members = lax.axis_size("beam"), lax.axis_size("trans")
    band, cols = field_in.shape[2:]
    rows = members * band
    inner = rows - 2 * (rows // 8)
    width = phases.shape[1] // SUBLANES
    lanes = -(-groups * members // LANES) * LANES
    table = jnp.asarray(one_axis_propagator(cols))
    vmem, hbm = (pl.BlockSpec(memory_space=space) for space in (pltpu.VMEM, pltpu.HBM))
    dma = pltpu.SemaphoreType.DMA
    made = pl.pallas_call(
        functools.partial(slices_kernel, groups),
        out_shape=(
            jax.ShapeDtypeStruct(field_in.shape, F32),
            jax.ShapeDtypeStruct(phases.shape, F32),
            jax.ShapeDtypeStruct(energy.shape, F32),
        ),
        in_specs=[hbm] * 11,
        out_specs=(hbm, vmem, vmem),
        scratch_shapes=[
            *[pltpu.VMEM(array.shape, array.dtype) for array in (phases, energy, row_cell, col_cell, weight)],
            *[pltpu.SMEM(array.shape, array.dtype) for array in (charge, pole_rate, pole_freq, pole_amp)],
            pltpu.VMEM((2, members, band, cols), F32),
            pltpu.VMEM((2, members, band, cols), F32),
            pltpu.VMEM(table.shape, BF16),
            pltpu.VMEM((2, 3, SUBLANES, width), F32),
            pltpu.VMEM((2, 2, SUBLANES, width), F32),
            pltpu.VMEM((2, SUBLANES, width), F32),
            pltpu.VMEM((members, 2, SUBLANES, width), F32),
            pltpu.VMEM((2, SUBLANES, width), F32),
            pltpu.VMEM((2, SUBLANES, width), F32),
            pltpu.VMEM((2, 2 * inner, cols), BF16),
            pltpu.VMEM((2, SUBLANES, cols, width), BF16),
            pltpu.VMEM((2, SUBLANES, width, cols), BF16),
            pltpu.VMEM(table.shape, BF16),
            pltpu.VMEM((2 * inner, SUBLANES * width), BF16),
            pltpu.VMEM((groups, SUBLANES, lanes), F32),
            pltpu.VMEM((SUBLANES, lanes), F32),
            dma((members,)), dma((members,)), dma, dma, dma, dma, dma((members,)), dma((members,)),
            dma((members,)), dma((members,)), dma((groups,)), dma((groups,)), dma((13,)),
        ],
        compiler_params=pltpu.CompilerParams(
            collective_id=0, has_side_effects=True, vmem_limit_bytes=VMEM_GRANT
        ),
    )(field_in, phases, energy, row_cell, col_cell, weight, charge, pole_rate, pole_freq, pole_amp, table)
    copies = 2 * members + 2
    return tuple(pl.pallas_call(
        settle_kernel,
        out_shape=tuple(jax.ShapeDtypeStruct(array.shape, F32) for array in made),
        in_specs=[hbm] * 3,
        out_specs=(hbm,) * 3,
        scratch_shapes=[dma((copies,))],
        compiler_params=pltpu.CompilerParams(vmem_limit_bytes=VMEM_GRANT),
    )(*made))


def pick_plan(field_in, *others):
    members = field_in.shape[1]
    whole = members == lax.axis_size("trans") and members % 2 == 0 and members >= 4 and lax.axis_size("beam") >= 3
    return (whole_slices if whole else shards)(field_in, *others)


def solution(mesh):
    placed = (
        P(None, "beam", "trans", None),
        P("beam", None),
        P("beam", None),
        P("beam", None),
        P("beam", None),
        P("beam", None),
        P("beam"),
        P(),
        P(),
        P(),
    )
    return jax.shard_map(
        pick_plan,
        mesh=mesh,
        in_specs=placed,
        out_specs=(P(None, "beam", "trans", None), P("beam", None), P("beam", None)),
        check_vma=False,
    )
```

```python
import functools
import math

import jax
import jax.numpy as jnp
import ml_dtypes
import numpy as np
from jax import lax
from jax.experimental import pallas as pl
from jax.experimental.pallas import tpu as pltpu
from jax.sharding import PartitionSpec as P

PERIODS = 2


diffraction = 20.0
kick_gain = 0.5
deposit_gain = 0.05
wake_gain = 3.0
charge_unit = 1024.0


def shifted(value, axis, steps):
    count = lax.axis_size(axis)
    first, last = (max(0, -steps), min(count, count - steps))
    return lax.ppermute(value, axis, [(source, source + steps) for source in range(first, last)])


def complex_product(form, left_re, left_im, right_re, right_im):

    def single(first, second):
        return jnp.einsum(form, first, second, precision=lax.Precision.HIGHEST)

    return (
        single(left_re, right_re) - single(left_im, right_im),
        single(left_re, right_im) + single(left_im, right_re),
    )


def dft_table(length, sign):
    counter = jnp.arange(length, dtype=jnp.int32)
    product = counter[:, None] * counter[None, :] % length
    radians = 2.0 * math.pi / length * product.astype(jnp.float32)
    factor = 1.0 / math.sqrt(length)
    return (jnp.cos(radians) * factor, sign * jnp.sin(radians) * factor)


def propagator(row_index, col_index, length):

    def centred(index):
        return ((index + length // 2) % length - length // 2).astype(jnp.float32) / length

    radians = diffraction * (centred(row_index) ** 2 + centred(col_index) ** 2)
    return (jnp.cos(radians), -jnp.sin(radians))


def pole_power(steps, pole_rate, pole_freq):
    damping = jnp.exp(-pole_rate * steps)
    radians = pole_freq * steps
    return (damping * jnp.cos(radians), damping * jnp.sin(radians))


def wake_kicks(charge, pole_rate, pole_freq, pole_amp):
    members = charge.shape[0]
    groups = lax.axis_size("beam")
    position = lax.axis_index("beam")
    charge_norm = charge.astype(jnp.float32) / charge_unit
    offsets = jnp.arange(members, dtype=jnp.float32)
    distance = offsets[:, None] - offsets[None, :]
    inner_re, inner_im = pole_power(jnp.maximum(distance, 0.0)[..., None], pole_rate, pole_freq)
    before = (distance > 0.0)[..., None]
    local_re = jnp.sum(jnp.where(before, inner_re, 0.0) * charge_norm[None, :, None], axis=1)
    tail_re, tail_im = pole_power((members - offsets)[:, None], pole_rate, pole_freq)
    block_re = jnp.sum(charge_norm[:, None] * tail_re, axis=0)
    block_im = jnp.sum(charge_norm[:, None] * tail_im, axis=0)
    gathered_re, gathered_im = (
        lax.all_gather(block_re[None, :], "beam", axis=0, tiled=True),
        lax.all_gather(block_im[None, :], "beam", axis=0, tiled=True),
    )
    sources = jnp.arange(groups, dtype=jnp.int32)
    spacing = (position - 1 - sources).astype(jnp.float32) * members
    reach_re, reach_im = pole_power(jnp.maximum(spacing, 0.0)[:, None], pole_rate, pole_freq)
    valid = (sources < position)[:, None]
    carry_re = jnp.sum(
        jnp.where(valid, gathered_re * reach_re - gathered_im * reach_im, 0.0), axis=0
    )
    carry_im = jnp.sum(
        jnp.where(valid, gathered_re * reach_im + gathered_im * reach_re, 0.0), axis=0
    )
    lead_re, lead_im = pole_power(offsets[:, None], pole_rate, pole_freq)
    state_re = local_re + lead_re * carry_re[None, :] - lead_im * carry_im[None, :]
    summed = jnp.sum(pole_amp[None, :] * (state_re + 0.5 * charge_norm[:, None]), axis=1)
    return wake_gain / (members * groups) * summed


def deposit_slice(band_rows, grid_cols, operands):
    local_row, column, part_re, part_im = operands
    row_hot = (local_row[:, None] == jnp.arange(band_rows, dtype=jnp.int32)[None, :]).astype(
        jnp.bfloat16
    )
    col_hot = (column[:, None] == jnp.arange(grid_cols, dtype=jnp.int32)[None, :]).astype(
        jnp.bfloat16
    )
    spread = jnp.concatenate([col_hot * part_re[:, None], col_hot * part_im[:, None]], axis=1)
    return lax.dot_general(
        row_hot, spread, (((0,), (0,)), ((), ())), preferred_element_type=jnp.float32
    )


def probe_slice(band_rows, grid_cols, operands):
    local_row, column, slab_re, slab_im = operands
    row_hot = (local_row[:, None] == jnp.arange(band_rows, dtype=jnp.int32)[None, :]).astype(
        jnp.float32
    )
    stacked = jnp.concatenate([slab_re, slab_im], axis=1)
    picked = jnp.dot(
        row_hot, stacked, precision=lax.Precision.HIGHEST, preferred_element_type=jnp.float32
    )
    col_hot = column[:, None] == jnp.arange(grid_cols, dtype=jnp.int32)[None, :]
    value_re = jnp.sum(jnp.where(col_hot, picked[:, :grid_cols], 0.0), axis=1)
    value_im = jnp.sum(jnp.where(col_hot, picked[:, grid_cols:], 0.0), axis=1)
    return (value_re, value_im)


def diffract(field_re, field_im, forward, inverse):
    cols_re, cols_im = complex_product("srn,nc->scr", field_re, field_im, forward[0], forward[1])
    halves = lax.all_to_all(
        jnp.stack([cols_re, cols_im]), "trans", split_axis=2, concat_axis=3, tiled=True
    )
    part_re = halves[0]
    part_im = halves[1]
    col_band = part_re.shape[1]
    grid_rows = part_re.shape[2]
    columns = lax.axis_index("trans") * col_band + jnp.arange(col_band, dtype=jnp.int32)
    spec_re, spec_im = complex_product("sqr,rk->sqk", part_re, part_im, forward[0], forward[1])
    kernel_re, kernel_im = propagator(
        jnp.arange(grid_rows, dtype=jnp.int32)[None, :], columns[:, None], grid_rows
    )
    moved_re = spec_re * kernel_re - spec_im * kernel_im
    moved_im = spec_re * kernel_im + spec_im * kernel_re
    back_re, back_im = complex_product("sqk,kr->sqr", moved_re, moved_im, inverse[0], inverse[1])
    rows_both = lax.all_to_all(
        jnp.stack([back_re, back_im]), "trans", split_axis=3, concat_axis=2, tiled=True
    )
    return complex_product("scr,cn->srn", rows_both[0], rows_both[1], inverse[0], inverse[1])


def shards(
    field_in, phases, energy, row_cell, col_cell, weight, charge, pole_rate, pole_freq, pole_amp
):
    field_re = field_in[0]
    field_im = field_in[1]
    slab_count, band_rows, grid_cols = field_re.shape
    row_start = lax.axis_index("trans") * band_rows
    wake_kick = wake_kicks(charge, pole_rate, pole_freq, pole_amp)
    charge_norm = charge.astype(jnp.float32) / charge_unit
    strength = (deposit_gain * charge_norm)[:, None, None]
    local_row = row_cell - row_start
    weights = weight.astype(jnp.float32)
    forward = dft_table(grid_cols, -1.0)
    inverse = dft_table(grid_cols, 1.0)
    depositor = functools.partial(deposit_slice, band_rows, grid_cols)
    reader = functools.partial(probe_slice, band_rows, grid_cols)
    angles = phases
    energies = energy
    for period in range(PERIODS):
        local_re, local_im = lax.map(reader, (local_row, col_cell, field_re, field_im))
        probed = lax.psum(jnp.stack([local_re, local_im]), "trans")
        energies = (
            energies
            - kick_gain * (probed[0] * jnp.cos(angles) - probed[1] * jnp.sin(angles))
            - wake_kick[:, None]
        )
        angles = angles + energies
        part_re = (weights * jnp.cos(angles)).astype(jnp.bfloat16)
        part_im = (-weights * jnp.sin(angles)).astype(jnp.bfloat16)
        bunched = lax.map(depositor, (local_row, col_cell, part_re, part_im))
        field_re = field_re + strength * bunched[:, :, :grid_cols]
        field_im = field_im + strength * bunched[:, :, grid_cols:]
        field_re, field_im = diffract(field_re, field_im, forward, inverse)
        head_slice = shifted(jnp.stack([field_re[-1], field_im[-1]]), "beam", 1)
        field_re = jnp.concatenate([head_slice[0][None], field_re[:-1]], axis=0)
        field_im = jnp.concatenate([head_slice[1][None], field_im[:-1]], axis=0)
    return (jnp.stack([field_re, field_im]), angles, energies)


MESH = pl.DeviceIdType.MESH
LANES = 128
SUBLANES = 8
VMEM_GRANT = 64 * 1024 * 1024 - 64 * 1024
F32 = jnp.float32
BF16 = jnp.bfloat16


def one_axis_propagator(length):
    index = np.arange(length)
    centred = ((index + length // 2) % length - length // 2) / length
    ring = np.fft.ifft(np.exp(-1j * diffraction * centred**2))
    full = ring[(index[:, None] - index[None, :]) % length]
    block = np.block([[full.real, -full.imag], [full.imag, full.real]]).astype(np.float32)
    upper = block.astype(ml_dtypes.bfloat16)
    lower = (block - upper.astype(np.float32)).astype(ml_dtypes.bfloat16)
    return np.stack([upper, lower])


def two_parts(value):
    upper = value.astype(BF16)
    return upper, (value - upper.astype(F32)).astype(BF16)


def mm(left, right):
    return jnp.dot(left, right, preferred_element_type=F32)


def mm_t(left, right):
    return lax.dot_general(left, right, (((1,), (1,)), ((), ())), preferred_element_type=F32)


def slices_kernel(
    groups,
    field_in, phases_in, energy_in, row_in, col_in, weight_in, charge_in, rate_in, freq_in, amp_in, table,
    field_out, phase_out, energy_out,
    phase_rows, energy_rows, phases, energy, row_cell, col_cell, weight, charge, pole_rate, pole_freq, pole_amp, field, moved, taps, cells, state, result, arrived, probes, parts, halves, col_hot, row_hot, charges, charge_tile,
    field_send, field_recv, cell_send, cell_recv, state_send, state_recv, result_send, result_recv,
    out_send, out_recv, charge_send, charge_recv, local_sems,
):
    beam, trans = lax.axis_index("beam"), lax.axis_index("trans")
    members, band, cols = field_in.shape[1:]
    rows = members * band
    total = groups * members
    half = members // 2
    width = phases.shape[1] // SUBLANES
    edge = rows // 8
    inner = rows - 2 * edge
    mine = beam * members + trans
    ahead, behind = lax.rem(beam + 1, groups), lax.rem(beam + groups - 1, groups)

    barrier = pltpu.get_barrier_semaphore()

    def greet(beam_to, trans_to):
        pl.semaphore_signal(barrier, inc=1, device_id=(beam_to, trans_to), device_id_type=MESH)

    for step in range(1, members):
        greet(beam, lax.rem(trans + step, members))
    for step in range(1, groups):
        greet(lax.rem(beam + step, groups), trans)
    for source in (members - 2, members - 1):
        @pl.when(trans != source)
        def _():
            greet(behind, source)

    @pl.when(trans == members - 1)
    def _():
        greet(ahead, 0)

    small = []
    for k, (source, target) in enumerate((
        (row_in, row_cell), (col_in, col_cell), (weight_in, weight), (phases_in, phases), (energy_in, energy),
        (charge_in, charge), (rate_in, pole_rate), (freq_in, pole_freq), (amp_in, pole_amp),
    )):
        small.append(pltpu.make_async_copy(source, target, local_sems.at[4 + k]))
        small[-1].start()
    take = pltpu.make_async_copy(field_in.at[:, trans], field.at[:, trans], local_sems.at[0])
    take.start()
    take_table = pltpu.make_async_copy(table, taps, local_sems.at[1])
    take_table.start()

    expected = (members - 1) + (groups - 1) + jnp.where(trans >= members - 2, members - 1, 0) + jnp.where(trans == 0, 1, 0)
    pl.semaphore_wait(barrier, expected)

    def remote(source, target, send, recv, beam_to, trans_to):
        return pltpu.make_async_remote_copy(
            src_ref=source, dst_ref=target, send_sem=send, recv_sem=recv,
            device_id=(beam_to, trans_to), device_id_type=MESH,
        )

    field_copies = []
    way = jnp.where(trans < half, 1, members - 1)
    for step in [half] + [k for k in range(1, members) if k != half]:
        to = lax.rem(trans + way * step, members)
        copy = remote(field_in.at[:, to], field.at[:, trans], field_send.at[step], field_recv.at[trans], beam, to)
        copy.start()
        field_copies.append(copy)

    for copy in small:
        copy.wait()

    lane = lax.broadcasted_iota(jnp.int32, charge_tile.shape, 1)
    own = jnp.zeros(charge_tile.shape, F32)
    for k in range(members):
        own = jnp.where(lane == beam * members + k, charge[k].astype(F32) / charge_unit, own)
    charge_tile[...] = own
    charges[pl.ds(beam, 1)] = own[None]
    charge_copies = []
    for step in range(1, groups):
        copy = remote(charge_tile, charges.at[beam], charge_send.at[step], charge_recv.at[beam], lax.rem(beam + step, groups), trans)
        copy.start()
        charge_copies.append(copy)

    for k in range(SUBLANES):
        here = pl.ds(k * width, width)
        for place, source in enumerate((row_cell, col_cell, weight)):
            cells[0, place, k : k + 1, :] = source[pl.ds(trans, 1), here].astype(F32)
        state[0, 0, k : k + 1, :] = phases[pl.ds(trans, 1), here]
        state[0, 1, k : k + 1, :] = energy[pl.ds(trans, 1), here]
    first = trans == 0
    prior_beam = jnp.where(first, behind, beam)
    prior_trans = jnp.where(first, members - 1, trans - 1)
    cell_copy = remote(cells.at[0], cells.at[1], cell_send, cell_recv, prior_beam, prior_trans)
    cell_copy.start()

    def one_hots(period):
        col_index = lax.broadcasted_iota(jnp.int32, (cols, width), 0).astype(F32)

        def body(k, carry):
            col_hot[period, k] = jnp.where(cells[period, 1, pl.ds(k, 1), :] == col_index, 1.0, 0.0).astype(BF16)
            return carry

        lax.fori_loop(0, SUBLANES, body, 0)

    one_hots(0)

    for step in range(1, groups):
        source = lax.rem(beam + step, groups)
        remote(charge_tile, charges.at[source], charge_send.at[step], charge_recv.at[source], source, trans).wait_recv()
    every = jnp.sum(charges[...], axis=0)

    def wake_and_charge(slice_id):
        distance = slice_id - lane
        ago = jnp.maximum(distance, 0).astype(F32)
        memory = jnp.zeros(lane.shape, F32)
        amount = F32(0)
        for k in range(pole_rate.shape[0]):
            memory = memory + pole_amp[k] * (jnp.exp(-pole_rate[k] * ago) * jnp.cos(pole_freq[k] * ago))
            amount = amount + pole_amp[k]
        memory = jnp.where(distance > 0, memory, jnp.where(distance == 0, 0.5 * amount, 0.0))
        wake = (wake_gain / total) * jnp.sum(memory * every, axis=1, keepdims=True)
        return wake, jnp.sum(jnp.where(distance == 0, every, 0.0), axis=1, keepdims=True)

    following = lax.rem(mine + 1, total)
    wakes = [wake_and_charge(mine), wake_and_charge(following)]
    cell_copy.wait_recv()
    one_hots(1)
    start_cos, start_sin = jnp.cos(state[0, 0]), jnp.sin(state[0, 0])

    row_index = lax.broadcasted_iota(jnp.int32, (inner, width), 0).astype(F32) + float(edge)

    def probe_band(source, opens):
        upper, lower = two_parts(field[:, source].reshape(2 * band, cols))
        band_index = (lax.broadcasted_iota(jnp.int32, (band, width), 0) + source * band).astype(F32)

        def body(k, carry):
            hot = col_hot[0, k]
            picked = mm(upper, hot) + mm(lower, hot)
            inside = cells[0, 0, pl.ds(k, 1), :] == band_index
            for part in range(2):
                found = jnp.sum(
                    jnp.where(inside, picked[part * band : (part + 1) * band], 0.0), axis=0, keepdims=True
                )
                probes[part, pl.ds(k, 1), :] = found if opens else probes[part, pl.ds(k, 1), :] + found
            return carry

        lax.fori_loop(0, SUBLANES, body, 0, unroll=True)

    def probe(period):
        flat = field[...].reshape(2, rows, cols)
        for part in range(2):
            upper, lower = two_parts(flat[part, edge : rows - edge])
            halves[0, part * inner : (part + 1) * inner, :] = upper
            halves[1, part * inner : (part + 1) * inner, :] = lower

        def body(k, carry):
            hot = col_hot[period, k]
            picked = mm(halves[0], hot) + mm(halves[1], hot)
            inside = cells[period, 0, pl.ds(k, 1), :] == row_index
            probes[0, pl.ds(k, 1), :] = jnp.sum(jnp.where(inside, picked[:inner], 0.0), axis=0, keepdims=True)
            probes[1, pl.ds(k, 1), :] = jnp.sum(jnp.where(inside, picked[inner:], 0.0), axis=0, keepdims=True)
            return carry

        lax.fori_loop(0, SUBLANES, body, 0, unroll=True)

    def push(period, cos_now, sin_now):
        eta = state[period, 1] - kick_gain * (probes[0] * cos_now - probes[1] * sin_now) - wakes[period][0]
        theta = state[period, 0] + eta
        return theta, eta

    def deposit(period, theta):
        heavy = cells[period, 2]
        parts[0] = (heavy * jnp.cos(theta)).astype(BF16).astype(F32)
        parts[1] = (-heavy * jnp.sin(theta)).astype(BF16).astype(F32)
        bunched = jnp.zeros((2 * inner, cols), F32)
        for k in range(SUBLANES):
            inside = cells[period, 0, k : k + 1, :] == row_index
            spread = jnp.concatenate(
                [jnp.where(inside, parts[part, k : k + 1, :], 0.0).astype(BF16) for part in range(2)], axis=0
            )
            row_hot[:, k * width : (k + 1) * width] = spread
            bunched = bunched + mm_t(row_hot[:, k * width : (k + 1) * width], col_hot[period, k])
        strength = deposit_gain * wakes[period][1][:1, :1]
        flat = field[...].reshape(2, rows, cols)
        wide = []
        for part in range(2):
            loaded = flat[part, edge : rows - edge] + strength * bunched[part * inner : (part + 1) * inner]
            wide.append(jnp.concatenate([flat[part, :edge], loaded, flat[part, rows - edge :]], axis=0))
        upper, lower = two_parts(jnp.concatenate(wide, axis=1))
        across = mm_t(upper, taps[0]) + (mm_t(lower, taps[0]) + mm_t(upper, taps[1]))
        return two_parts(jnp.concatenate([across[:, :cols], across[:, cols:]], axis=0))

    def along_rows(first_row, count, upper, lower):
        here = [pl.ds(pl.multiple_of(part * rows + first_row, band), count) for part in range(2)]
        major, minor = (jnp.concatenate([taps[part, where] for where in here], axis=0) for part in range(2))
        return (mm(major, upper) + (mm(major, lower) + mm(minor, upper))).reshape(2, count, cols)

    take.wait()
    probe_band(trans, True)
    for step in range(1, members):
        source = lax.rem(trans + way * step, members)
        remote(field_in.at[:, source], field.at[:, source], field_send.at[step], field_recv.at[source], beam, source).wait_recv()
        probe_band(source, False)
    take_table.wait()
    theta, eta = push(0, start_cos, start_sin)
    state[0, 0] = theta
    state[0, 1] = eta
    state_copy = remote(state.at[0], state.at[1], state_send, state_recv, prior_beam, prior_trans)
    state_copy.start()
    turned = along_rows(0, rows, *deposit(0, theta))
    field[...] = jnp.where(following == 0, 0.0, turned).reshape(field.shape)

    state_copy.wait_recv()
    probe(1)
    theta, eta = push(1, jnp.cos(state[1, 0]), jnp.sin(state[1, 0]))
    result[0] = theta
    result[1] = eta

    def scatter(shift, source_of, target, send, recv, sem):
        slot = lax.rem(trans + shift, members)
        stays = trans + shift < members
        beam_to = jnp.where(stays, beam, ahead)

        def away(to):
            return remote(source_of(to), target(slot), send.at[to], recv.at[slot], beam_to, to)

        def here():
            return pltpu.make_async_copy(source_of(trans), target(slot), sem)

        def start(to):
            same = jnp.logical_and(stays, to == trans)

            @pl.when(same)
            def _():
                here().start()

            @pl.when(jnp.logical_not(same))
            def _():
                away(to).start()

        def finish():
            for to in range(members):
                @pl.when(jnp.logical_not(jnp.logical_and(stays, to == trans)))
                def _():
                    away(to).wait_send()

            @pl.when(stays)
            def _():
                here().wait()

            for place in range(members):
                def wait_for():
                    remote(source_of(trans), target(place), send.at[0], recv.at[place], beam, trans).wait_recv()

                if place < shift:
                    wait_for()
                else:
                    pl.when(trans != place - shift)(wait_for)

        return start, finish

    start_result, finish_result = scatter(
        1, lambda to: result, lambda slot: arrived.at[slot], result_send, result_recv, local_sems.at[2]
    )
    for to in range(members):
        start_result(to)
    upper, lower = deposit(1, theta)
    start_field, finish_field = scatter(
        2, lambda to: moved.at[:, to], lambda slot: field_out.at[:, slot], out_send, out_recv, local_sems.at[3]
    )
    mine_half = trans // half
    for side in (1 - mine_half, mine_half):
        turned = along_rows(side * (half * band), half * band, upper, lower)
        turned = jnp.where(lax.rem(mine + 2, total) == 0, 0.0, turned)
        for k in range(half):
            moved[:, side * half + k] = turned[:, k * band : (k + 1) * band]
            start_field(side * half + k)

    finish_result()
    for place in range(members):
        for k in range(SUBLANES):
            here = slice(k * width, (k + 1) * width)
            phase_rows[place : place + 1, here] = arrived[place, 0, k : k + 1, :]
            energy_rows[place : place + 1, here] = arrived[place, 1, k : k + 1, :]
    leaving = [
        pltpu.make_async_copy(phase_rows, phase_out, local_sems.at[13]),
        pltpu.make_async_copy(energy_rows, energy_out, local_sems.at[14]),
    ]
    for copy in leaving:
        copy.start()
    for copy in field_copies + charge_copies + [cell_copy, state_copy]:
        copy.wait_send()
    finish_field()
    for copy in leaving:
        copy.wait()


def settle_kernel(
    field_made, phase_made, energy_made, field_out, phase_out, energy_out, field, phase, energy, in_sems, out_sems
):
    pieces = [(phase_made, phase, phase_out), (energy_made, energy, energy_out)]
    for part in range(2):
        for place in range(field_made.shape[1]):
            pieces.append(tuple(ref.at[part, place] for ref in (field_made, field, field_out)))
    loads = [pltpu.make_async_copy(made, held, in_sems.at[k]) for k, (made, held, _) in enumerate(pieces)]
    stores = [pltpu.make_async_copy(held, out, out_sems.at[k]) for k, (_, held, out) in enumerate(pieces)]
    for load in loads:
        load.start()
    for load, store in zip(loads, stores):
        load.wait()
        store.start()
    for store in stores:
        store.wait()


def whole_slices(
    field_in, phases, energy, row_cell, col_cell, weight, charge, pole_rate, pole_freq, pole_amp
):
    groups, members = lax.axis_size("beam"), lax.axis_size("trans")
    band, cols = field_in.shape[2:]
    rows = members * band
    inner = rows - 2 * (rows // 8)
    width = phases.shape[1] // SUBLANES
    lanes = -(-groups * members // LANES) * LANES
    table = jnp.asarray(one_axis_propagator(cols))
    hbm = pl.BlockSpec(memory_space=pltpu.HBM)
    dma = pltpu.SemaphoreType.DMA
    made = pl.pallas_call(
        functools.partial(slices_kernel, groups),
        out_shape=(
            jax.ShapeDtypeStruct(field_in.shape, F32),
            jax.ShapeDtypeStruct(phases.shape, F32),
            jax.ShapeDtypeStruct(energy.shape, F32),
        ),
        in_specs=[hbm] * 11,
        out_specs=(hbm,) * 3,
        scratch_shapes=[
            *[pltpu.VMEM(array.shape, array.dtype) for array in (phases, energy, phases, energy, row_cell, col_cell, weight)],
            *[pltpu.SMEM(array.shape, array.dtype) for array in (charge, pole_rate, pole_freq, pole_amp)],
            pltpu.VMEM((2, members, band, cols), F32),
            pltpu.VMEM((2, members, band, cols), F32),
            pltpu.VMEM(table.shape, BF16),
            pltpu.VMEM((2, 3, SUBLANES, width), F32),
            pltpu.VMEM((2, 2, SUBLANES, width), F32),
            pltpu.VMEM((2, SUBLANES, width), F32),
            pltpu.VMEM((members, 2, SUBLANES, width), F32),
            pltpu.VMEM((2, SUBLANES, width), F32),
            pltpu.VMEM((2, SUBLANES, width), F32),
            pltpu.VMEM((2, 2 * inner, cols), BF16),
            pltpu.VMEM((2, SUBLANES, cols, width), BF16),
            pltpu.VMEM((2 * inner, SUBLANES * width), BF16),
            pltpu.VMEM((groups, SUBLANES, lanes), F32),
            pltpu.VMEM((SUBLANES, lanes), F32),
            dma((members,)), dma((members,)), dma, dma, dma, dma, dma((members,)), dma((members,)),
            dma((members,)), dma((members,)), dma((groups,)), dma((groups,)), dma((15,)),
        ],
        compiler_params=pltpu.CompilerParams(
            collective_id=0, has_side_effects=True, vmem_limit_bytes=VMEM_GRANT
        ),
    )(field_in, phases, energy, row_cell, col_cell, weight, charge, pole_rate, pole_freq, pole_amp, table)
    copies = 2 * members + 2
    return tuple(pl.pallas_call(
        settle_kernel,
        out_shape=tuple(jax.ShapeDtypeStruct(array.shape, F32) for array in made),
        in_specs=[hbm] * 3,
        out_specs=(hbm,) * 3,
        scratch_shapes=[*[pltpu.VMEM(array.shape, F32) for array in made], dma((copies,)), dma((copies,))],
        compiler_params=pltpu.CompilerParams(vmem_limit_bytes=VMEM_GRANT),
    )(*made))


def pick_plan(field_in, *others):
    members = field_in.shape[1]
    whole = members == lax.axis_size("trans") and members % 2 == 0 and members >= 4 and lax.axis_size("beam") >= 3
    return (whole_slices if whole else shards)(field_in, *others)


def solution(mesh):
    placed = (
        P(None, "beam", "trans", None),
        P("beam", None),
        P("beam", None),
        P("beam", None),
        P("beam", None),
        P("beam", None),
        P("beam"),
        P(),
        P(),
        P(),
    )
    return jax.shard_map(
        pick_plan,
        mesh=mesh,
        in_specs=placed,
        out_specs=(P(None, "beam", "trans", None), P("beam", None), P("beam", None)),
        check_vma=False,
    )
```

```python
import functools
import math

import jax
import jax.numpy as jnp
import ml_dtypes
import numpy as np
from jax import lax
from jax.experimental import pallas as pl
from jax.experimental.pallas import tpu as pltpu
from jax.sharding import PartitionSpec as P

PERIODS = 2


diffraction = 20.0
kick_gain = 0.5
deposit_gain = 0.05
wake_gain = 3.0
charge_unit = 1024.0


def shifted(value, axis, steps):
    count = lax.axis_size(axis)
    first, last = (max(0, -steps), min(count, count - steps))
    return lax.ppermute(value, axis, [(source, source + steps) for source in range(first, last)])


def complex_product(form, left_re, left_im, right_re, right_im):

    def single(first, second):
        return jnp.einsum(form, first, second, precision=lax.Precision.HIGHEST)

    return (
        single(left_re, right_re) - single(left_im, right_im),
        single(left_re, right_im) + single(left_im, right_re),
    )


def dft_table(length, sign):
    counter = jnp.arange(length, dtype=jnp.int32)
    product = counter[:, None] * counter[None, :] % length
    radians = 2.0 * math.pi / length * product.astype(jnp.float32)
    factor = 1.0 / math.sqrt(length)
    return (jnp.cos(radians) * factor, sign * jnp.sin(radians) * factor)


def propagator(row_index, col_index, length):

    def centred(index):
        return ((index + length // 2) % length - length // 2).astype(jnp.float32) / length

    radians = diffraction * (centred(row_index) ** 2 + centred(col_index) ** 2)
    return (jnp.cos(radians), -jnp.sin(radians))


def pole_power(steps, pole_rate, pole_freq):
    damping = jnp.exp(-pole_rate * steps)
    radians = pole_freq * steps
    return (damping * jnp.cos(radians), damping * jnp.sin(radians))


def wake_kicks(charge, pole_rate, pole_freq, pole_amp):
    members = charge.shape[0]
    groups = lax.axis_size("beam")
    position = lax.axis_index("beam")
    charge_norm = charge.astype(jnp.float32) / charge_unit
    offsets = jnp.arange(members, dtype=jnp.float32)
    distance = offsets[:, None] - offsets[None, :]
    inner_re, inner_im = pole_power(jnp.maximum(distance, 0.0)[..., None], pole_rate, pole_freq)
    before = (distance > 0.0)[..., None]
    local_re = jnp.sum(jnp.where(before, inner_re, 0.0) * charge_norm[None, :, None], axis=1)
    tail_re, tail_im = pole_power((members - offsets)[:, None], pole_rate, pole_freq)
    block_re = jnp.sum(charge_norm[:, None] * tail_re, axis=0)
    block_im = jnp.sum(charge_norm[:, None] * tail_im, axis=0)
    gathered_re, gathered_im = (
        lax.all_gather(block_re[None, :], "beam", axis=0, tiled=True),
        lax.all_gather(block_im[None, :], "beam", axis=0, tiled=True),
    )
    sources = jnp.arange(groups, dtype=jnp.int32)
    spacing = (position - 1 - sources).astype(jnp.float32) * members
    reach_re, reach_im = pole_power(jnp.maximum(spacing, 0.0)[:, None], pole_rate, pole_freq)
    valid = (sources < position)[:, None]
    carry_re = jnp.sum(
        jnp.where(valid, gathered_re * reach_re - gathered_im * reach_im, 0.0), axis=0
    )
    carry_im = jnp.sum(
        jnp.where(valid, gathered_re * reach_im + gathered_im * reach_re, 0.0), axis=0
    )
    lead_re, lead_im = pole_power(offsets[:, None], pole_rate, pole_freq)
    state_re = local_re + lead_re * carry_re[None, :] - lead_im * carry_im[None, :]
    summed = jnp.sum(pole_amp[None, :] * (state_re + 0.5 * charge_norm[:, None]), axis=1)
    return wake_gain / (members * groups) * summed


def deposit_slice(band_rows, grid_cols, operands):
    local_row, column, part_re, part_im = operands
    row_hot = (local_row[:, None] == jnp.arange(band_rows, dtype=jnp.int32)[None, :]).astype(
        jnp.bfloat16
    )
    col_hot = (column[:, None] == jnp.arange(grid_cols, dtype=jnp.int32)[None, :]).astype(
        jnp.bfloat16
    )
    spread = jnp.concatenate([col_hot * part_re[:, None], col_hot * part_im[:, None]], axis=1)
    return lax.dot_general(
        row_hot, spread, (((0,), (0,)), ((), ())), preferred_element_type=jnp.float32
    )


def probe_slice(band_rows, grid_cols, operands):
    local_row, column, slab_re, slab_im = operands
    row_hot = (local_row[:, None] == jnp.arange(band_rows, dtype=jnp.int32)[None, :]).astype(
        jnp.float32
    )
    stacked = jnp.concatenate([slab_re, slab_im], axis=1)
    picked = jnp.dot(
        row_hot, stacked, precision=lax.Precision.HIGHEST, preferred_element_type=jnp.float32
    )
    col_hot = column[:, None] == jnp.arange(grid_cols, dtype=jnp.int32)[None, :]
    value_re = jnp.sum(jnp.where(col_hot, picked[:, :grid_cols], 0.0), axis=1)
    value_im = jnp.sum(jnp.where(col_hot, picked[:, grid_cols:], 0.0), axis=1)
    return (value_re, value_im)


def diffract(field_re, field_im, forward, inverse):
    cols_re, cols_im = complex_product("srn,nc->scr", field_re, field_im, forward[0], forward[1])
    halves = lax.all_to_all(
        jnp.stack([cols_re, cols_im]), "trans", split_axis=2, concat_axis=3, tiled=True
    )
    part_re = halves[0]
    part_im = halves[1]
    col_band = part_re.shape[1]
    grid_rows = part_re.shape[2]
    columns = lax.axis_index("trans") * col_band + jnp.arange(col_band, dtype=jnp.int32)
    spec_re, spec_im = complex_product("sqr,rk->sqk", part_re, part_im, forward[0], forward[1])
    kernel_re, kernel_im = propagator(
        jnp.arange(grid_rows, dtype=jnp.int32)[None, :], columns[:, None], grid_rows
    )
    moved_re = spec_re * kernel_re - spec_im * kernel_im
    moved_im = spec_re * kernel_im + spec_im * kernel_re
    back_re, back_im = complex_product("sqk,kr->sqr", moved_re, moved_im, inverse[0], inverse[1])
    rows_both = lax.all_to_all(
        jnp.stack([back_re, back_im]), "trans", split_axis=3, concat_axis=2, tiled=True
    )
    return complex_product("scr,cn->srn", rows_both[0], rows_both[1], inverse[0], inverse[1])


def shards(
    field_in, phases, energy, row_cell, col_cell, weight, charge, pole_rate, pole_freq, pole_amp
):
    field_re = field_in[0]
    field_im = field_in[1]
    slab_count, band_rows, grid_cols = field_re.shape
    row_start = lax.axis_index("trans") * band_rows
    wake_kick = wake_kicks(charge, pole_rate, pole_freq, pole_amp)
    charge_norm = charge.astype(jnp.float32) / charge_unit
    strength = (deposit_gain * charge_norm)[:, None, None]
    local_row = row_cell - row_start
    weights = weight.astype(jnp.float32)
    forward = dft_table(grid_cols, -1.0)
    inverse = dft_table(grid_cols, 1.0)
    depositor = functools.partial(deposit_slice, band_rows, grid_cols)
    reader = functools.partial(probe_slice, band_rows, grid_cols)
    angles = phases
    energies = energy
    for period in range(PERIODS):
        local_re, local_im = lax.map(reader, (local_row, col_cell, field_re, field_im))
        probed = lax.psum(jnp.stack([local_re, local_im]), "trans")
        energies = (
            energies
            - kick_gain * (probed[0] * jnp.cos(angles) - probed[1] * jnp.sin(angles))
            - wake_kick[:, None]
        )
        angles = angles + energies
        part_re = (weights * jnp.cos(angles)).astype(jnp.bfloat16)
        part_im = (-weights * jnp.sin(angles)).astype(jnp.bfloat16)
        bunched = lax.map(depositor, (local_row, col_cell, part_re, part_im))
        field_re = field_re + strength * bunched[:, :, :grid_cols]
        field_im = field_im + strength * bunched[:, :, grid_cols:]
        field_re, field_im = diffract(field_re, field_im, forward, inverse)
        head_slice = shifted(jnp.stack([field_re[-1], field_im[-1]]), "beam", 1)
        field_re = jnp.concatenate([head_slice[0][None], field_re[:-1]], axis=0)
        field_im = jnp.concatenate([head_slice[1][None], field_im[:-1]], axis=0)
    return (jnp.stack([field_re, field_im]), angles, energies)


MESH = pl.DeviceIdType.MESH
LANES = 128
SUBLANES = 8
VMEM_GRANT = 64 * 1024 * 1024 - 64 * 1024
F32 = jnp.float32
BF16 = jnp.bfloat16


def one_axis_propagator(length):
    index = np.arange(length)
    centred = ((index + length // 2) % length - length // 2) / length
    ring = np.fft.ifft(np.exp(-1j * diffraction * centred**2))
    full = ring[(index[:, None] - index[None, :]) % length]
    block = np.block([[full.real, -full.imag], [full.imag, full.real]]).astype(np.float32)
    upper = block.astype(ml_dtypes.bfloat16)
    lower = (block - upper.astype(np.float32)).astype(ml_dtypes.bfloat16)
    return np.stack([upper, lower])


def two_parts(value):
    upper = value.astype(BF16)
    return upper, (value - upper.astype(F32)).astype(BF16)


def mm(left, right):
    return jnp.dot(left, right, preferred_element_type=F32)


def mm_t(left, right):
    return lax.dot_general(left, right, (((1,), (1,)), ((), ())), preferred_element_type=F32)


def slices_kernel(
    groups,
    field_in, phases_in, energy_in, row_in, col_in, weight_in, charge_in, rate_in, freq_in, amp_in, table,
    field_out, phase_out, energy_out,
    phase_rows, energy_rows, phases, energy, row_cell, col_cell, weight, charge, pole_rate, pole_freq, pole_amp, field, moved, taps, cells, state, result, arrived, probes, parts, halves, col_hot, taps_t, row_hot, charges, charge_tile,
    field_send, field_recv, cell_send, cell_recv, state_send, state_recv, result_send, result_recv,
    out_send, out_recv, charge_send, charge_recv, local_sems,
):
    beam, trans = lax.axis_index("beam"), lax.axis_index("trans")
    members, band, cols = field_in.shape[1:]
    rows = members * band
    total = groups * members
    half = members // 2
    width = phases.shape[1] // SUBLANES
    edge = rows // 8
    inner = rows - 2 * edge
    mine = beam * members + trans
    ahead, behind = lax.rem(beam + 1, groups), lax.rem(beam + groups - 1, groups)

    barrier = pltpu.get_barrier_semaphore()

    def greet(beam_to, trans_to):
        pl.semaphore_signal(barrier, inc=1, device_id=(beam_to, trans_to), device_id_type=MESH)

    for step in range(1, members):
        greet(beam, lax.rem(trans + step, members))
    for step in range(1, groups):
        greet(lax.rem(beam + step, groups), trans)
    for source in (members - 2, members - 1):
        @pl.when(trans != source)
        def _():
            greet(behind, source)

    @pl.when(trans == members - 1)
    def _():
        greet(ahead, 0)

    small = []
    for k, (source, target) in enumerate((
        (row_in, row_cell), (col_in, col_cell), (weight_in, weight), (phases_in, phases), (energy_in, energy),
        (charge_in, charge), (rate_in, pole_rate), (freq_in, pole_freq), (amp_in, pole_amp),
    )):
        small.append(pltpu.make_async_copy(source, target, local_sems.at[4 + k]))
        small[-1].start()
    take = pltpu.make_async_copy(field_in.at[:, trans], field.at[:, trans], local_sems.at[0])
    take.start()
    take_table = pltpu.make_async_copy(table, taps, local_sems.at[1])
    take_table.start()

    expected = (members - 1) + (groups - 1) + jnp.where(trans >= members - 2, members - 1, 0) + jnp.where(trans == 0, 1, 0)
    pl.semaphore_wait(barrier, expected)

    def remote(source, target, send, recv, beam_to, trans_to):
        return pltpu.make_async_remote_copy(
            src_ref=source, dst_ref=target, send_sem=send, recv_sem=recv,
            device_id=(beam_to, trans_to), device_id_type=MESH,
        )

    field_copies = []
    way = jnp.where(trans < half, 1, members - 1)
    mine_half = trans // half
    beyond = [(1 - mine_half) * half + lax.rem(trans + k, half) for k in range(half)]
    nearby = [mine_half * half + lax.rem(trans + k, half) for k in range(1, half)]
    for to in beyond + nearby:
        copy = remote(field_in.at[:, to], field.at[:, trans], field_send.at[to], field_recv.at[trans], beam, to)
        copy.start()
        field_copies.append(copy)

    for copy in small:
        copy.wait()

    lane = lax.broadcasted_iota(jnp.int32, charge_tile.shape, 1)
    own = jnp.zeros(charge_tile.shape, F32)
    for k in range(members):
        own = jnp.where(lane == beam * members + k, charge[k].astype(F32) / charge_unit, own)
    charge_tile[...] = own
    charges[pl.ds(beam, 1)] = own[None]
    charge_copies = []
    for step in range(1, groups):
        copy = remote(charge_tile, charges.at[beam], charge_send.at[step], charge_recv.at[beam], lax.rem(beam + step, groups), trans)
        copy.start()
        charge_copies.append(copy)

    for k in range(SUBLANES):
        here = pl.ds(k * width, width)
        for place, source in enumerate((row_cell, col_cell, weight)):
            cells[0, place, k : k + 1, :] = source[pl.ds(trans, 1), here].astype(F32)
        state[0, 0, k : k + 1, :] = phases[pl.ds(trans, 1), here]
        state[0, 1, k : k + 1, :] = energy[pl.ds(trans, 1), here]
    first = trans == 0
    prior_beam = jnp.where(first, behind, beam)
    prior_trans = jnp.where(first, members - 1, trans - 1)
    cell_copy = remote(cells.at[0], cells.at[1], cell_send, cell_recv, prior_beam, prior_trans)
    cell_copy.start()

    def one_hots(period):
        col_index = lax.broadcasted_iota(jnp.int32, (cols, width), 0).astype(F32)

        def body(k, carry):
            col_hot[period, k] = jnp.where(cells[period, 1, pl.ds(k, 1), :] == col_index, 1.0, 0.0).astype(BF16)
            return carry

        lax.fori_loop(0, SUBLANES, body, 0)

    one_hots(0)

    for step in range(1, groups):
        source = lax.rem(beam + step, groups)
        remote(charge_tile, charges.at[source], charge_send.at[step], charge_recv.at[source], source, trans).wait_recv()
    every = jnp.sum(charges[...], axis=0)

    def wake_and_charge(slice_id):
        distance = slice_id - lane
        ago = jnp.maximum(distance, 0).astype(F32)
        memory = jnp.zeros(lane.shape, F32)
        amount = F32(0)
        for k in range(pole_rate.shape[0]):
            memory = memory + pole_amp[k] * (jnp.exp(-pole_rate[k] * ago) * jnp.cos(pole_freq[k] * ago))
            amount = amount + pole_amp[k]
        memory = jnp.where(distance > 0, memory, jnp.where(distance == 0, 0.5 * amount, 0.0))
        wake = (wake_gain / total) * jnp.sum(memory * every, axis=1, keepdims=True)
        return wake, jnp.sum(jnp.where(distance == 0, every, 0.0), axis=1, keepdims=True)

    following = lax.rem(mine + 1, total)
    wakes = [wake_and_charge(mine), wake_and_charge(following)]
    cell_copy.wait_recv()
    one_hots(1)
    start_cos, start_sin = jnp.cos(state[0, 0]), jnp.sin(state[0, 0])

    row_index = lax.broadcasted_iota(jnp.int32, (inner, width), 0).astype(F32) + float(edge)

    def probe_band(source, opens):
        upper, lower = two_parts(field[:, source].reshape(2 * band, cols))
        band_index = (lax.broadcasted_iota(jnp.int32, (band, width), 0) + source * band).astype(F32)

        def body(k, carry):
            hot = col_hot[0, k]
            picked = mm(upper, hot) + mm(lower, hot)
            inside = cells[0, 0, pl.ds(k, 1), :] == band_index
            for part in range(2):
                found = jnp.sum(
                    jnp.where(inside, picked[part * band : (part + 1) * band], 0.0), axis=0, keepdims=True
                )
                probes[part, pl.ds(k, 1), :] = found if opens else probes[part, pl.ds(k, 1), :] + found
            return carry

        lax.fori_loop(0, SUBLANES, body, 0, unroll=True)

    def probe(period):
        flat = field[...].reshape(2, rows, cols)
        for part in range(2):
            upper, lower = two_parts(flat[part, edge : rows - edge])
            halves[0, part * inner : (part + 1) * inner, :] = upper
            halves[1, part * inner : (part + 1) * inner, :] = lower

        def body(k, carry):
            hot = col_hot[period, k]
            picked = mm(halves[0], hot) + mm(halves[1], hot)
            inside = cells[period, 0, pl.ds(k, 1), :] == row_index
            probes[0, pl.ds(k, 1), :] = jnp.sum(jnp.where(inside, picked[:inner], 0.0), axis=0, keepdims=True)
            probes[1, pl.ds(k, 1), :] = jnp.sum(jnp.where(inside, picked[inner:], 0.0), axis=0, keepdims=True)
            return carry

        lax.fori_loop(0, SUBLANES, body, 0, unroll=True)

    def push(period, cos_now, sin_now):
        eta = state[period, 1] - kick_gain * (probes[0] * cos_now - probes[1] * sin_now) - wakes[period][0]
        theta = state[period, 0] + eta
        return theta, eta

    def deposit(period, theta):
        heavy = cells[period, 2]
        parts[0] = (heavy * jnp.cos(theta)).astype(BF16).astype(F32)
        parts[1] = (-heavy * jnp.sin(theta)).astype(BF16).astype(F32)
        bunched = jnp.zeros((2 * inner, cols), F32)
        for k in range(SUBLANES):
            inside = cells[period, 0, k : k + 1, :] == row_index
            spread = jnp.concatenate(
                [jnp.where(inside, parts[part, k : k + 1, :], 0.0).astype(BF16) for part in range(2)], axis=0
            )
            row_hot[:, k * width : (k + 1) * width] = spread
            bunched = bunched + mm_t(row_hot[:, k * width : (k + 1) * width], col_hot[period, k])
        strength = deposit_gain * wakes[period][1][:1, :1]
        flat = field[...].reshape(2, rows, cols)
        wide = []
        for part in range(2):
            loaded = flat[part, edge : rows - edge] + strength * bunched[part * inner : (part + 1) * inner]
            wide.append(jnp.concatenate([flat[part, :edge], loaded, flat[part, rows - edge :]], axis=0))
        upper, lower = two_parts(jnp.concatenate(wide, axis=1))
        across = mm(upper, taps_t[0]) + (mm(lower, taps_t[0]) + mm(upper, taps_t[1]))
        return two_parts(jnp.concatenate([across[:, :cols], across[:, cols:]], axis=0))

    def along_rows(first_row, count, upper, lower):
        here = [pl.ds(pl.multiple_of(part * rows + first_row, band), count) for part in range(2)]
        major, minor = (jnp.concatenate([taps[part, where] for where in here], axis=0) for part in range(2))
        return (mm(major, upper) + (mm(major, lower) + mm(minor, upper))).reshape(2, count, cols)

    take_table.wait()
    for part in range(2):
        both = taps[part]
        taps_t[part, :cols] = jnp.concatenate([both[:cols, :cols], both[cols:, :cols]], axis=1)
        taps_t[part, cols:] = jnp.concatenate([both[:cols, cols:], both[cols:, cols:]], axis=1)
    take.wait()
    probe_band(trans, True)
    for step in range(1, members):
        source = lax.rem(trans + way * step, members)
        remote(field_in.at[:, source], field.at[:, source], field_send.at[source], field_recv.at[source], beam, source).wait_recv()
        probe_band(source, False)
    theta, eta = push(0, start_cos, start_sin)
    state[0, 0] = theta
    state[0, 1] = eta
    state_copy = remote(state.at[0], state.at[1], state_send, state_recv, prior_beam, prior_trans)
    state_copy.start()
    turned = along_rows(0, rows, *deposit(0, theta))
    field[...] = jnp.where(following == 0, 0.0, turned).reshape(field.shape)

    state_copy.wait_recv()
    probe(1)
    theta, eta = push(1, jnp.cos(state[1, 0]), jnp.sin(state[1, 0]))
    result[0] = theta
    result[1] = eta

    def scatter(shift, source_of, target, send, recv, sem):
        slot = lax.rem(trans + shift, members)
        stays = trans + shift < members
        beam_to = jnp.where(stays, beam, ahead)

        def away(to):
            return remote(source_of(to), target(slot), send.at[to], recv.at[slot], beam_to, to)

        def here():
            return pltpu.make_async_copy(source_of(trans), target(slot), sem)

        def start(to):
            same = jnp.logical_and(stays, to == trans)

            @pl.when(same)
            def _():
                here().start()

            @pl.when(jnp.logical_not(same))
            def _():
                away(to).start()

        def finish():
            for to in range(members):
                @pl.when(jnp.logical_not(jnp.logical_and(stays, to == trans)))
                def _():
                    away(to).wait_send()

            @pl.when(stays)
            def _():
                here().wait()

            for place in range(members):
                def wait_for():
                    remote(source_of(trans), target(place), send.at[0], recv.at[place], beam, trans).wait_recv()

                if place < shift:
                    wait_for()
                else:
                    pl.when(trans != place - shift)(wait_for)

        return start, finish

    start_result, finish_result = scatter(
        1, lambda to: result, lambda slot: arrived.at[slot], result_send, result_recv, local_sems.at[2]
    )
    for to in range(members):
        start_result(to)
    upper, lower = deposit(1, theta)
    start_field, finish_field = scatter(
        2, lambda to: moved.at[:, to], lambda slot: field_out.at[:, slot], out_send, out_recv, local_sems.at[3]
    )
    for side in (1 - mine_half, mine_half):
        turned = along_rows(side * (half * band), half * band, upper, lower)
        turned = jnp.where(lax.rem(mine + 2, total) == 0, 0.0, turned)
        for k in range(half):
            moved[:, side * half + k] = turned[:, k * band : (k + 1) * band]
            start_field(side * half + k)

    finish_result()
    for place in range(members):
        for k in range(SUBLANES):
            here = slice(k * width, (k + 1) * width)
            phase_rows[place : place + 1, here] = arrived[place, 0, k : k + 1, :]
            energy_rows[place : place + 1, here] = arrived[place, 1, k : k + 1, :]
    leaving = [
        pltpu.make_async_copy(phase_rows, phase_out, local_sems.at[13]),
        pltpu.make_async_copy(energy_rows, energy_out, local_sems.at[14]),
    ]
    for copy in leaving:
        copy.start()
    for copy in field_copies + charge_copies + [cell_copy, state_copy]:
        copy.wait_send()
    finish_field()
    for copy in leaving:
        copy.wait()


def settle_kernel(
    field_made, phase_made, energy_made, field_out, phase_out, energy_out, field, phase, energy, in_sems, out_sems
):
    pieces = [(phase_made, phase, phase_out), (energy_made, energy, energy_out)]
    for part in range(2):
        for place in range(field_made.shape[1]):
            pieces.append(tuple(ref.at[part, place] for ref in (field_made, field, field_out)))
    loads = [pltpu.make_async_copy(made, held, in_sems.at[k]) for k, (made, held, _) in enumerate(pieces)]
    stores = [pltpu.make_async_copy(held, out, out_sems.at[k]) for k, (_, held, out) in enumerate(pieces)]
    for load in loads:
        load.start()
    for load, store in zip(loads, stores):
        load.wait()
        store.start()
    for store in stores:
        store.wait()


def whole_slices(
    field_in, phases, energy, row_cell, col_cell, weight, charge, pole_rate, pole_freq, pole_amp
):
    groups, members = lax.axis_size("beam"), lax.axis_size("trans")
    band, cols = field_in.shape[2:]
    rows = members * band
    inner = rows - 2 * (rows // 8)
    width = phases.shape[1] // SUBLANES
    lanes = -(-groups * members // LANES) * LANES
    table = jnp.asarray(one_axis_propagator(cols))
    hbm = pl.BlockSpec(memory_space=pltpu.HBM)
    dma = pltpu.SemaphoreType.DMA
    made = pl.pallas_call(
        functools.partial(slices_kernel, groups),
        out_shape=(
            jax.ShapeDtypeStruct(field_in.shape, F32),
            jax.ShapeDtypeStruct(phases.shape, F32),
            jax.ShapeDtypeStruct(energy.shape, F32),
        ),
        in_specs=[hbm] * 11,
        out_specs=(hbm,) * 3,
        scratch_shapes=[
            *[pltpu.VMEM(array.shape, array.dtype) for array in (phases, energy, phases, energy, row_cell, col_cell, weight)],
            *[pltpu.SMEM(array.shape, array.dtype) for array in (charge, pole_rate, pole_freq, pole_amp)],
            pltpu.VMEM((2, members, band, cols), F32),
            pltpu.VMEM((2, members, band, cols), F32),
            pltpu.VMEM(table.shape, BF16),
            pltpu.VMEM((2, 3, SUBLANES, width), F32),
            pltpu.VMEM((2, 2, SUBLANES, width), F32),
            pltpu.VMEM((2, SUBLANES, width), F32),
            pltpu.VMEM((members, 2, SUBLANES, width), F32),
            pltpu.VMEM((2, SUBLANES, width), F32),
            pltpu.VMEM((2, SUBLANES, width), F32),
            pltpu.VMEM((2, 2 * inner, cols), BF16),
            pltpu.VMEM((2, SUBLANES, cols, width), BF16),
            pltpu.VMEM(table.shape, BF16),
            pltpu.VMEM((2 * inner, SUBLANES * width), BF16),
            pltpu.VMEM((groups, SUBLANES, lanes), F32),
            pltpu.VMEM((SUBLANES, lanes), F32),
            dma((members,)), dma((members,)), dma, dma, dma, dma, dma((members,)), dma((members,)),
            dma((members,)), dma((members,)), dma((groups,)), dma((groups,)), dma((15,)),
        ],
        compiler_params=pltpu.CompilerParams(
            collective_id=0, has_side_effects=True, vmem_limit_bytes=VMEM_GRANT
        ),
    )(field_in, phases, energy, row_cell, col_cell, weight, charge, pole_rate, pole_freq, pole_amp, table)
    copies = 2 * members + 2
    return tuple(pl.pallas_call(
        settle_kernel,
        out_shape=tuple(jax.ShapeDtypeStruct(array.shape, F32) for array in made),
        in_specs=[hbm] * 3,
        out_specs=(hbm,) * 3,
        scratch_shapes=[*[pltpu.VMEM(array.shape, F32) for array in made], dma((copies,)), dma((copies,))],
        compiler_params=pltpu.CompilerParams(vmem_limit_bytes=VMEM_GRANT),
    )(*made))


def pick_plan(field_in, *others):
    members = field_in.shape[1]
    whole = members == lax.axis_size("trans") and members % 2 == 0 and members >= 4 and lax.axis_size("beam") >= 3
    return (whole_slices if whole else shards)(field_in, *others)


def solution(mesh):
    placed = (
        P(None, "beam", "trans", None),
        P("beam", None),
        P("beam", None),
        P("beam", None),
        P("beam", None),
        P("beam", None),
        P("beam"),
        P(),
        P(),
        P(),
    )
    return jax.shard_map(
        pick_plan,
        mesh=mesh,
        in_specs=placed,
        out_specs=(P(None, "beam", "trans", None), P("beam", None), P("beam", None)),
        check_vma=False,
    )
```
